512 devices in a mesh: row: 16 (over z, core), col: 4 (over y_hi), rep: 8 (over y_lo, x).
Axes of the slice: x: 4, y: 8 (y_hi: 4, y_lo: 2; y = y_hi * 2 + y_lo), z: 8, core: 2. Of those that a mesh axis runs over, the one named last changes fastest.
Arguments:
- features: bfloat16 [65536, 128], P(('row', 'col', 'rep')), may hold values from -6 to 6
- weight_in: bfloat16 [128, 128], replicated, may hold values from -0.5 to 0.5
- weight_hidden: bfloat16 [128, 128], replicated, may hold values from -0.5 to 0.5
- tile_rows: int32 [16, 32, 96], P('row', ('col', 'rep')), may hold values from 0 to 31
- tile_cols: int32 [16, 32, 96], P('row', ('col', 'rep')), may hold values from 0 to 15
- tile_values: bfloat16 [16, 32, 96, 128, 128], P('row', ('col', 'rep')), may hold values from -0.5 to 0.5
- tile_counts: int32 [16, 32], P('row', ('col', 'rep')), may hold values from 48 to 96, as said below
- cotangent: bfloat16 [65536, 128], P(('row', 'col', 'rep')), may hold values from -0.0234375 to 0.0234375
Outputs:
- logits: float32 [65536, 128], P(('row', 'col', 'rep'))
- grad_weight_in: float32 [128, 128], replicated
- grad_weight_hidden: float32 [128, 128], replicated
The draws below stay inside these ranges and needn't reach their ends.
Inputs may be any that keep to these rules, and one draw needn't show every extreme that they name: `tile_rows`: only an owner's live slots count; the data in the other slots is arbitrary. Two live slots may name the same tile row and column; their tiles add. `tile_counts`: in every draw some owner has all 96 slots live.
All inputs are finite; a program needn't handle non-finite values.
Results may differ from the reference program's by a relative error of at most 0.04.
Values may be sent and summed in bfloat16 or wider, within the bound.
A program may use at most 64 MiB of HBM per device.

```python
import jax
import jax.numpy as jnp
from jax import lax

F_IN = 128
HID = 128
TILE = 128
NODE_DEV = 128
TMAX = 96
GROUP = 32
NODES = 65536
ROW_BLOCKS = 32
COL_BLOCKS = 16
N_ROW = 16
N_COL = 4
N_REP = 8


def draw_tile_counts(key, part):
    key = jax.random.fold_in(key, 7)
    base_key, heavy_key = jax.random.split(key)
    owners = N_ROW * GROUP
    base_counts = jax.random.randint(base_key, (owners,), TMAX // 2, TMAX + 1)
    heavy_owner = jax.random.randint(heavy_key, (), 0, owners)
    base_counts = base_counts.at[heavy_owner].set(TMAX)
    return base_counts.reshape(N_ROW, GROUP).astype(jnp.int32)


def plant(result, key, least, largest):
    dims = result.shape
    index_at = [jax.random.randint(jax.random.fold_in(key, axis), (), 0, dims[axis]) for axis in range(len(dims))]
    result = result.at[tuple(index_at)].set(least)
    longest = dims.index(max(dims))
    index_at[longest] = (index_at[longest] + 1) % dims[longest]
    return result.at[tuple(index_at)].set(largest)


def shard_levels(rng, dims, shards, smallest, largest):
    def one(dim, blocks):
        steps = jax.random.uniform(jax.random.fold_in(jax.random.fold_in(rng, 6), dim), (blocks,), jnp.float32, smallest / len(shards), largest / len(shards))
        return jnp.repeat(jnp.exp(steps), dims[dim] // blocks).reshape((-1,) + (1,) * (len(dims) - dim - 1))

    loudness = one(*shards[0])
    for cut in shards[1:]:
        loudness = loudness * one(*cut)
    return loudness


def centred(key, dims, spread, most, shards=(), held_as=jnp.bfloat16):
    values = jax.random.normal(key, dims, jnp.float32) * spread
    if len(shards) > 0:
        values = shard_levels(key, dims, shards, -0.22, 0.18) * values
    return jnp.clip(values, min=-most, max=most).astype(held_as)


def setup_inputs(seed: int = 0) -> dict:
    key_list = jax.random.split(jax.random.key(seed), 9)
    features = centred(key_list[0], (NODES, F_IN), 1.0, 6.0, ((0, 512),))
    weight_in = centred(key_list[1], (F_IN, HID), F_IN ** -0.5, 0.5)
    weight_hidden = centred(key_list[2], (HID, HID), HID ** -0.5, 0.5)
    tile_rows = plant(jax.random.randint(key_list[3], (N_ROW, GROUP, TMAX), 0, ROW_BLOCKS), jax.random.fold_in(key_list[3], 1), 0, ROW_BLOCKS - 1).astype(jnp.int32)
    tile_cols = plant(jax.random.randint(key_list[4], (N_ROW, GROUP, TMAX), 0, COL_BLOCKS), jax.random.fold_in(key_list[4], 1), 0, COL_BLOCKS - 1).astype(jnp.int32)
    tile_values = centred(key_list[5], (N_ROW, GROUP, TMAX, TILE, TILE), TILE ** -0.5, 0.5, ((0, 16), (1, 32)))
    tile_counts = draw_tile_counts(jax.random.fold_in(key_list[8], 71), 0)
    cotangent = centred(key_list[7], (NODES, HID), (NODES ** -0.5), 0.0234375, ((0, 512),))
    return {"features": features, "weight_in": weight_in, "weight_hidden": weight_hidden, "tile_rows": tile_rows, "tile_cols": tile_cols, "tile_values": tile_values, "tile_counts": tile_counts, "cotangent": cotangent}


def reference(features, weight_in, weight_hidden, tile_rows, tile_cols, tile_values, tile_counts, cotangent):
    group_count = N_COL * N_REP
    owners = N_ROW * group_count
    row_blocks = group_count * NODE_DEV // TILE
    col_blocks = N_ROW * NODE_DEV // TILE
    all_values = tile_values.reshape(owners, TMAX, TILE, TILE)
    all_rows = tile_rows.reshape(owners, TMAX)
    all_cols = tile_cols.reshape(owners, TMAX)
    all_counts = tile_counts.reshape(owners)
    owner_ids = jnp.arange(owners, dtype=jnp.int32)
    slot_ids = jnp.arange(TMAX, dtype=jnp.int32)

    def forward_sum(source):
        node_grid = source.reshape(N_ROW, group_count, NODE_DEV, HID)

        def visit_owner(running, owner_data):
            owner_index, tile_block, row_index, col_index, tile_count = owner_data
            row_group = owner_index // group_count
            col_group = owner_index % group_count
            column = lax.dynamic_index_in_dim(node_grid, col_group, 1, keepdims=False).reshape(col_blocks, TILE, HID)
            picked = column[col_index].astype(jnp.float32)
            live_mask = (slot_ids < tile_count).astype(jnp.float32)
            products = jnp.einsum("tij,tjh->tih", tile_block.astype(jnp.float32), picked) * live_mask[:, None, None]
            partial_value = jax.ops.segment_sum(products, row_index, num_segments=row_blocks)
            partial_value = lax.optimization_barrier(partial_value.astype(jnp.bfloat16)).astype(jnp.float32)
            return running.at[row_group].add(partial_value.reshape(group_count * NODE_DEV, HID)), None

        start_sum = jnp.zeros((N_ROW, group_count * NODE_DEV, HID), jnp.float32)
        running, unused = lax.scan(visit_owner, start_sum, (owner_ids, all_values, all_rows, all_cols, all_counts))
        return running.reshape(owners * NODE_DEV, HID)

    def backward_sum(source):
        node_grid = source.reshape(N_ROW, group_count * NODE_DEV, HID)

        def visit_owner(running, owner_data):
            owner_index, tile_block, row_index, col_index, tile_count = owner_data
            row_group = owner_index // group_count
            col_group = owner_index % group_count
            row_range = lax.dynamic_index_in_dim(node_grid, row_group, 0, keepdims=False).reshape(row_blocks, TILE, HID)
            picked = row_range[row_index].astype(jnp.float32)
            live_mask = (slot_ids < tile_count).astype(jnp.float32)
            products = jnp.einsum("tji,tjh->tih", tile_block.astype(jnp.float32), picked) * live_mask[:, None, None]
            partial_value = jax.ops.segment_sum(products, col_index, num_segments=col_blocks)
            partial_value = lax.optimization_barrier(partial_value.astype(jnp.bfloat16)).astype(jnp.float32)
            return running.at[:, col_group].add(partial_value.reshape(N_ROW, NODE_DEV, HID)), None

        start_sum = jnp.zeros((N_ROW, group_count, NODE_DEV, HID), jnp.float32)
        running, unused = lax.scan(visit_owner, start_sum, (owner_ids, all_values, all_rows, all_cols, all_counts))
        return running.reshape(owners * NODE_DEV, HID)

    products_first = jnp.dot(features, weight_in, preferred_element_type=jnp.float32).astype(jnp.bfloat16)
    sum_first = forward_sum(products_first)
    hidden = jax.nn.silu(sum_first).astype(jnp.bfloat16)
    products_second = jnp.dot(hidden, weight_hidden, preferred_element_type=jnp.float32).astype(jnp.bfloat16)
    logits = forward_sum(products_second)
    grad_products_second = backward_sum(cotangent).astype(jnp.bfloat16)
    grad_weight_hidden = jnp.dot(hidden.T, grad_products_second, preferred_element_type=jnp.float32)
    grad_hidden = jnp.dot(grad_products_second, weight_hidden.T, preferred_element_type=jnp.float32)
    gate_value = jax.nn.sigmoid(sum_first)
    grad_sum_first = (grad_hidden * gate_value * (1.0 + sum_first * (1.0 - gate_value))).astype(jnp.bfloat16)
    grad_products_first = backward_sum(grad_sum_first).astype(jnp.bfloat16)
    grad_weight_in = jnp.dot(features.T, grad_products_first, preferred_element_type=jnp.float32)
    return logits, grad_weight_in, grad_weight_hidden
```

```python
import functools

import jax
import jax.numpy as jnp
from jax import lax
from jax.experimental import pallas as pl
from jax.experimental.pallas import tpu as pltpu
from jax.sharding import PartitionSpec as P

MESH = pl.DeviceIdType.MESH
BF = jnp.bfloat16
F32 = jnp.float32
CONTRACT_LAST = (((1,), (1,)), ((), ()))


def ring_order(n):
    return sorted(range(1, n), key=lambda d: (min(d, n - d), d))


def kernel(
    nx, ny, nz, slots,
    meta, feat, w_in, w_hid, cot, tiles_hbm,
    logits, gw_in, gw_hid,
    tiles, col_src_0, col_src_1, row_src_0, row_src_1, part, send_f, rx_a, rx_b, mid_a, mid_b, ry_a, ry_b,
    send_b, r_core, mid_z, r_z, term, ar_row, ar_x, ar_y, ar_out,
    local_sem, ssem, rsem,
):
    row = lax.axis_index("row")
    col = lax.axis_index("col")
    rep = lax.axis_index("rep")
    reps_y = lax.axis_size("rep") // nx
    z, core = row // 2, row % 2
    y, x = col * reps_y + rep // nx, rep % nx

    def device(xx, yy, zz, cc):
        return (zz * 2 + cc, yy // reps_y, (yy % reps_y) * nx + xx)

    x_peers = [((x + d) % nx, device((x + d) % nx, y, z, core)) for d in ring_order(nx)]
    y_peers = [((y + d) % ny, device(x, (y + d) % ny, z, core)) for d in ring_order(ny)]
    z_peers = [((z + d) % nz, device(x, y, (z + d) % nz, core)) for d in ring_order(nz)]
    sibling = device(x, y, z, 1 - core)
    cross_peers = [((z + d) % nz, device(x, y, (z + d) % nz, 1 - core)) for d in ring_order(nz)]

    height = feat.shape[0]
    col_src, row_src = (col_src_0, col_src_1), (row_src_0, row_src_1)
    cut = 80

    tile_copy = pltpu.make_async_copy(tiles_hbm, tiles, local_sem.at[0])
    tile_copy.start()

    barrier = pltpu.get_barrier_semaphore()
    everyone = [p[1] for p in x_peers + y_peers + z_peers + cross_peers] + [sibling]
    for peer in everyone:
        pl.semaphore_signal(barrier, inc=1, device_id=peer, device_id_type=MESH)

    sends = []

    def push(phase, src, dst, peer):
        copy = pltpu.make_async_remote_copy(
            src_ref=src, dst_ref=dst, send_sem=ssem.at[phase], recv_sem=rsem.at[phase],
            device_id=peer, device_id_type=MESH,
        )
        copy.start()

    def landed(phase, ref):
        pltpu.make_async_copy(ref, ref, rsem.at[phase]).wait()

    def sent(phase, ref):
        sends.append((phase, ref))

    def gather_col_start(rnd, value):
        buf = col_src[rnd]
        buf[z, core] = value
        for _, peer in z_peers:
            push(rnd * 16 + 0, buf.at[z, core], buf.at[z, core], peer)
        sent(rnd * 16 + 0, buf.at[0 : nz - 1, 0])

    def gather_col_finish(rnd):
        buf = col_src[rnd]
        landed(rnd * 16 + 0, buf.at[0 : nz - 1, 0])
        push(rnd * 16 + 1, buf.at[:, core], buf.at[:, core], sibling)
        sent(rnd * 16 + 1, buf.at[:, 0])
        landed(rnd * 16 + 1, buf.at[:, 0])

    low, high = pl.ds(0, cut), pl.ds(cut, height - cut)

    def gather_row_start(rnd, value):
        buf = row_src[rnd]
        buf[y, x] = value
        for _, peer in y_peers:
            push(rnd * 16 + 2, buf.at[y, x, low], buf.at[y, x, low], peer)
        sent(rnd * 16 + 2, buf.at[0 : ny - 1, 0, low])
        for _, peer in x_peers:
            push(rnd * 16 + 3, buf.at[y, x, high], buf.at[y, x, high], peer)
        sent(rnd * 16 + 3, buf.at[0, 0 : nx - 1, high])

    def gather_row_second(rnd):
        buf = row_src[rnd]
        landed(rnd * 16 + 3, buf.at[0, 0 : nx - 1, high])
        for _, peer in y_peers:
            push(rnd * 16 + 5, buf.at[y, :, high], buf.at[y, :, high], peer)
        sent(rnd * 16 + 5, buf.at[0 : ny - 1, :, high])
        landed(rnd * 16 + 2, buf.at[0 : ny - 1, 0, low])
        for _, peer in x_peers:
            push(rnd * 16 + 4, buf.at[:, x, low], buf.at[:, x, low], peer)
        sent(rnd * 16 + 4, buf.at[:, 0 : nx - 1, low])

    def gather_row_finish(rnd):
        buf = row_src[rnd]
        landed(rnd * 16 + 5, buf.at[0 : ny - 1, :, high])
        landed(rnd * 16 + 4, buf.at[:, 0 : nx - 1, low])

    unroll = 8

    def spread_forward(rnd):
        src = col_src[rnd]

        def some(turn, acc):
            for i in range(unroll):
                k = turn * unroll + i
                c = meta[1, k]
                d = jnp.dot(tiles[meta[0, k]], src[c // 2, c % 2], preferred_element_type=F32)
                acc = jnp.where(meta[2, k] > 0, d, acc + d)
                part[k] = acc.astype(BF)
            return acc

        lax.fori_loop(0, slots // unroll, some, jnp.zeros((height, height), F32))

        def place(b, _):
            send_f[rnd, b // nx, b % nx] = part[meta[3, b]]
            return 0

        lax.fori_loop(0, nx * ny, place, 0)

    def spread_backward(rnd):
        src = row_src[rnd]

        def some(turn, acc):
            for i in range(unroll):
                k = turn * unroll + i
                r = meta[5, k]
                d = jnp.dot(src[r // nx, r % nx], tiles[meta[4, k]], preferred_element_type=F32)
                acc = jnp.where(meta[6, k] > 0, d, acc + d)
                part[k] = acc.astype(BF)
            return acc

        lax.fori_loop(0, slots // unroll, some, jnp.zeros((height, height), F32))

        def place(b, _):
            send_b[rnd, b // 2, b % 2] = part[meta[7, b]]
            return 0

        lax.fori_loop(0, nz * 2, place, 0)

    def reduce_rows_start(rnd):
        buf = send_f.at[rnd]
        for px, peer in x_peers:
            push(rnd * 16 + 6, buf.at[:, px, low], rx_a.at[rnd, x], peer)
        sent(rnd * 16 + 6, rx_a.at[rnd, 0 : nx - 1])
        for py, peer in y_peers:
            push(rnd * 16 + 7, buf.at[py, :, high], ry_b.at[rnd, y], peer)
        sent(rnd * 16 + 7, ry_b.at[rnd, 0 : ny - 1])

    def reduce_rows_second(rnd):
        buf = send_f.at[rnd]
        rx_a[rnd, x] = buf[:, x, 0:cut]
        ry_b[rnd, y] = buf[y, :, cut:height]
        landed(rnd * 16 + 6, rx_a.at[rnd, 0 : nx - 1])

        def add_x(b, _):
            total = rx_a[rnd, 0, b].astype(F32)
            for i in range(1, nx):
                total += rx_a[rnd, i, b].astype(F32)
            mid_a[rnd, b] = total.astype(BF)
            return 0

        lax.fori_loop(0, ny, add_x, 0)
        for py, peer in y_peers:
            push(rnd * 16 + 8, mid_a.at[rnd, py], ry_a.at[rnd, y], peer)
        sent(rnd * 16 + 8, ry_a.at[rnd, 0 : ny - 1])
        landed(rnd * 16 + 7, ry_b.at[rnd, 0 : ny - 1])

        def add_y(b, _):
            total = ry_b[rnd, 0, b].astype(F32)
            for i in range(1, ny):
                total += ry_b[rnd, i, b].astype(F32)
            mid_b[rnd, b] = total.astype(BF)
            return 0

        lax.fori_loop(0, nx, add_y, 0)
        for px, peer in x_peers:
            push(rnd * 16 + 9, mid_b.at[rnd, px], rx_b.at[rnd, x], peer)
        sent(rnd * 16 + 9, rx_b.at[rnd, 0 : nx - 1])
        ry_a[rnd, y] = mid_a[rnd, y]
        rx_b[rnd, x] = mid_b[rnd, x]

    def reduce_rows_finish(rnd):
        landed(rnd * 16 + 8, ry_a.at[rnd, 0 : ny - 1])
        top = ry_a[rnd, 0].astype(F32)
        for i in range(1, ny):
            top += ry_a[rnd, i].astype(F32)
        landed(rnd * 16 + 9, rx_b.at[rnd, 0 : nx - 1])
        bottom = rx_b[rnd, 0].astype(F32)
        for i in range(1, nx):
            bottom += rx_b[rnd, i].astype(F32)
        return jnp.concatenate([top, bottom], axis=0)

    def reduce_cols_start(rnd):
        buf = send_b.at[rnd]
        push(rnd * 16 + 10, buf.at[:, 1 - core], r_core.at[rnd], sibling)
        sent(rnd * 16 + 10, r_core.at[rnd])

    def reduce_cols_second(rnd):
        landed(rnd * 16 + 10, r_core.at[rnd])

        def add(b, _):
            mid_z[rnd, b] = (
                send_b[rnd, b, core].astype(F32) + r_core[rnd, b].astype(F32)
            ).astype(BF)
            return 0

        lax.fori_loop(0, nz, add, 0)
        for pz, peer in z_peers:
            push(rnd * 16 + 11, mid_z.at[rnd, pz], r_z.at[rnd, z], peer)
        sent(rnd * 16 + 11, r_z.at[rnd, 0 : nz - 1])
        r_z[rnd, z] = mid_z[rnd, z]

    def reduce_cols_finish(rnd):
        landed(rnd * 16 + 11, r_z.at[rnd, 0 : nz - 1])
        total = r_z[rnd, 0].astype(F32)
        for i in range(1, nz):
            total += r_z[rnd, i].astype(F32)
        return total.astype(BF)

    part[slots] = jnp.zeros((height, height), BF)
    products = jnp.dot(feat[...], w_in[...], preferred_element_type=F32).astype(BF)
    cot_t = cot[...].astype(F32).T.astype(BF)
    feat_t = feat[...].astype(F32).T.astype(BF)

    pl.semaphore_wait(barrier, len(everyone))

    gather_row_start(0, cot_t)
    gather_col_start(0, products)
    gather_row_second(0)
    gather_col_finish(0)
    tile_copy.wait()
    spread_forward(0)
    reduce_rows_start(0)
    gather_row_finish(0)
    spread_backward(0)
    reduce_cols_start(0)
    reduce_rows_second(0)
    reduce_cols_second(0)
    sum_first = reduce_rows_finish(0)
    gate = 1.0 / (1.0 + jnp.exp(-sum_first))
    hidden = (sum_first * gate).astype(BF)
    products = jnp.dot(hidden, w_hid[...], preferred_element_type=F32).astype(BF)
    gather_col_start(1, products)
    sum_t = sum_first.T
    gate_t = 1.0 / (1.0 + jnp.exp(-sum_t))
    hidden_t = (sum_t * gate_t).astype(BF)
    grad_t = reduce_cols_finish(0)
    grad_hidden_t = jnp.dot(w_hid[...], grad_t, preferred_element_type=F32)
    grad_sum_t = (grad_hidden_t * gate_t * (1.0 + sum_t * (1.0 - gate_t))).astype(BF)

    gather_row_start(1, grad_sum_t)
    term[1] = lax.dot_general(hidden_t, grad_t, CONTRACT_LAST, preferred_element_type=F32)
    gather_row_second(1)
    gather_col_finish(1)
    spread_forward(1)
    reduce_rows_start(1)
    gather_row_finish(1)
    spread_backward(1)
    reduce_cols_start(1)
    reduce_cols_second(1)
    reduce_rows_second(1)
    grad_first_t = reduce_cols_finish(1)
    term[0] = lax.dot_general(feat_t, grad_first_t, CONTRACT_LAST, preferred_element_type=F32)

    band = height // (2 * nz)
    row_peers = [(pz * 2 + core, peer) for pz, peer in z_peers]
    row_peers += [(pz * 2 + 1 - core, peer) for pz, peer in cross_peers]
    row_peers += [(z * 2 + 1 - core, sibling)]

    def rows_of(i):
        return pl.ds(pl.multiple_of(i * band, band), band)

    for i, peer in row_peers:
        push(12, term.at[:, rows_of(i)], ar_row.at[row], peer)
    sent(12, ar_row.at[0 : 2 * nz - 1])
    ar_row[row] = term[:, rows_of(row)]
    logits[...] = reduce_rows_finish(1)
    landed(12, ar_row.at[0 : 2 * nz - 1])
    total = ar_row[0]
    for i in range(1, 2 * nz):
        total += ar_row[i]
    ar_x[x] = total
    for _, peer in x_peers:
        push(13, ar_x.at[x], ar_x.at[x], peer)
    sent(13, ar_x.at[0 : nx - 1])
    landed(13, ar_x.at[0 : nx - 1])
    total = ar_x[0]
    for i in range(1, nx):
        total += ar_x[i]
    ar_y[y] = total
    for _, peer in y_peers:
        push(14, ar_y.at[y], ar_y.at[y], peer)
    sent(14, ar_y.at[0 : ny - 1])
    landed(14, ar_y.at[0 : ny - 1])
    total = ar_y[0]
    for i in range(1, ny):
        total += ar_y[i]
    ar_out[:, rows_of(row)] = total
    for _, peer in row_peers:
        push(15, ar_out.at[:, rows_of(row)], ar_out.at[:, rows_of(row)], peer)
    sent(15, ar_out.at[:, 0 : height - band])
    landed(15, ar_out.at[:, 0 : height - band])
    gw_in[...] = ar_out[0]
    gw_hid[...] = ar_out[1]

    for phase, ref in sends:
        pltpu.make_async_copy(ref, ref, ssem.at[phase]).wait()


def slot_order(group, other, count, groups, slots):
    at = jnp.arange(slots, dtype=jnp.int32)
    live = at < count
    key = jnp.where(live, group, groups)
    before = (key[None, :] < key[:, None]) | ((key[None, :] == key[:, None]) & (at[None, :] < at[:, None]))
    rank = jnp.sum(before, axis=1, dtype=jnp.int32)
    opens = jnp.logical_not(jnp.any((key[None, :] == key[:, None]) & (at[None, :] < at[:, None]), axis=1))
    here = rank[None, :] == at[:, None]
    values = jnp.stack([at, jnp.where(live, other, 0), opens.astype(jnp.int32)])
    placed = jnp.sum(jnp.where(here[None], values[:, None, :], 0), axis=2, dtype=jnp.int32)
    each = jnp.arange(groups, dtype=jnp.int32)
    upto = jnp.sum(key[None, :] <= each[:, None], axis=1, dtype=jnp.int32)
    found = jnp.any(key[None, :] == each[:, None], axis=1)
    last = jnp.where(found, upto - 1, slots)
    placed = jnp.pad(placed, ((0, 0), (0, 128 - slots)))
    return jnp.concatenate([placed, jnp.pad(last, (0, 128 - groups))[None]], axis=0)


def body(nx, features, weight_in, weight_hidden, tile_rows, tile_cols, tile_values, tile_counts, cotangent):
    nz = lax.axis_size("row") // 2
    ny = lax.axis_size(("col", "rep")) // nx
    slots, height = tile_values.shape[2], tile_values.shape[3]
    rows, cols, count = tile_rows[0, 0], tile_cols[0, 0], tile_counts[0, 0]
    meta = jnp.concatenate(
        [slot_order(rows, cols, count, nx * ny, slots), slot_order(cols, rows, count, nz * 2, slots)], axis=0
    )
    cut = 80
    rest = height - cut
    band = height // (2 * nz)
    block = (height, height)
    vmem = pl.BlockSpec(memory_space=pltpu.VMEM)
    return pl.pallas_call(
        functools.partial(kernel, nx, ny, nz, slots),
        out_shape=[jax.ShapeDtypeStruct(block, F32)] * 3,
        in_specs=[pl.BlockSpec(memory_space=pltpu.SMEM), vmem, vmem, vmem, vmem, pl.BlockSpec(memory_space=pl.ANY)],
        out_specs=[vmem] * 3,
        scratch_shapes=[
            pltpu.VMEM((slots,) + block, BF),
            pltpu.VMEM((nz, 2) + block, BF),
            pltpu.VMEM((nz, 2) + block, BF),
            pltpu.VMEM((ny, nx) + block, BF),
            pltpu.VMEM((ny, nx) + block, BF),
            pltpu.VMEM((slots + 1,) + block, BF),
            pltpu.VMEM((2, ny, nx) + block, BF),
            pltpu.VMEM((2, nx, ny, cut, height), BF),
            pltpu.VMEM((2, nx, rest, height), BF),
            pltpu.VMEM((2, ny, cut, height), BF),
            pltpu.VMEM((2, nx, rest, height), BF),
            pltpu.VMEM((2, ny, cut, height), BF),
            pltpu.VMEM((2, ny, nx, rest, height), BF),
            pltpu.VMEM((2, nz, 2) + block, BF),
            pltpu.VMEM((2, nz) + block, BF),
            pltpu.VMEM((2, nz) + block, BF),
            pltpu.VMEM((2, nz) + block, BF),
            pltpu.VMEM((2,) + block, F32),
            pltpu.VMEM((2 * nz, 2, band, height), F32),
            pltpu.VMEM((nx, 2, band, height), F32),
            pltpu.VMEM((ny, 2, band, height), F32),
            pltpu.VMEM((2,) + block, F32),
            pltpu.SemaphoreType.DMA((1,)),
            pltpu.SemaphoreType.DMA((32,)),
            pltpu.SemaphoreType.DMA((32,)),
        ],
        compiler_params=pltpu.CompilerParams(
            collective_id=0, has_side_effects=True, vmem_limit_bytes=48 * 1024 * 1024
        ),
    )(meta, features, weight_in, weight_hidden, cotangent, tile_values[0, 0])


def solution(mesh, nx=4):
    return jax.shard_map(
        functools.partial(body, nx),
        mesh=mesh,
        in_specs=(
            P(("row", "col", "rep"), None),
            P(),
            P(),
            P("row", ("col", "rep"), None),
            P("row", ("col", "rep"), None),
            P("row", ("col", "rep"), None, None, None),
            P("row", ("col", "rep")),
            P(("row", "col", "rep"), None),
        ),
        out_specs=(P(("row", "col", "rep"), None), P(), P()),
        check_vma=False,
    )
```

```python
import functools

import jax
import jax.numpy as jnp
from jax import lax
from jax.experimental import pallas as pl
from jax.experimental.pallas import tpu as pltpu
from jax.sharding import PartitionSpec as P

MESH = pl.DeviceIdType.MESH
BF = jnp.bfloat16
F32 = jnp.float32
I32 = jnp.int32
CONTRACT_LAST = (((1,), (1,)), ((), ()))
CUT = 96


def near_first(n):
    return sorted(range(1, n), key=lambda d: (min(d, n - d), d))


def far_first(n):
    return near_first(n)[::-1]


def split_dot(wide, weight):
    head = wide.astype(BF)
    rest = (wide - head.astype(F32)).astype(BF)
    return jnp.dot(head, weight, preferred_element_type=F32) + jnp.dot(rest, weight, preferred_element_type=F32)


def slot_order(group, other, count, groups):
    slots = group.shape[1]
    down = lax.broadcasted_iota(I32, (slots, slots), 0)
    along = lax.broadcasted_iota(I32, (slots, slots), 1)
    live = along < count

    def upright(row):
        return jnp.sum(jnp.where(down == along, row, 0), axis=1, keepdims=True)

    key = jnp.where(live, jnp.broadcast_to(group, (slots, slots)), groups)
    key_down = upright(key)
    other_down = upright(jnp.where(live, jnp.broadcast_to(other, (slots, slots)), 0))
    ahead = jnp.where((key == key_down) & (along < down), 1, 0)
    rank = jnp.sum(jnp.where(key < key_down, 1, ahead), axis=1, keepdims=True)
    opens = jnp.where(jnp.sum(ahead, axis=1, keepdims=True) == 0, 1, 0)
    here = rank == along

    def placed(value):
        return jnp.sum(jnp.where(here, value, 0), axis=0, keepdims=True)

    upto = jnp.sum(jnp.where(key_down <= along, 1, 0), axis=0, keepdims=True)
    found = jnp.sum(jnp.where(key_down == along, 1, 0), axis=0, keepdims=True)
    last = jnp.where(found > 0, upto - 1, slots)
    return placed(down), placed(other_down), placed(opens), last


def kernel(
    nx, ny, nz, slots,
    feat_hbm, w_in_hbm, w_hid_hbm, rows_hbm, cols_hbm, tiles_hbm, count_hbm, cot_hbm,
    logits, gw_in, gw_hid,
    w_in, w_hid, rows, cols, tiles, count, cot, meta_v, meta,
    col_src_0, col_src_1, row_src, part, send_f, rx_a, rx_b, mid_a, mid_b, ry_a, ry_b,
    send_b, r_core, mid_z, r_z, term, ar_row, ar_x, ar_y, ar_out,
    local_sem, ssem, rsem,
):
    row = lax.axis_index("row")
    col = lax.axis_index("col")
    rep = lax.axis_index("rep")
    reps_y = lax.axis_size("rep") // nx
    z, core = row // 2, row % 2
    y, x = col * reps_y + rep // nx, rep % nx
    height = cot.shape[0]
    low, high = pl.ds(0, CUT), pl.ds(CUT, height - CUT)
    col_src = (col_src_0, col_src_1)

    def device(xx, yy, zz, cc):
        return (zz * 2 + cc, yy // reps_y, (yy % reps_y) * nx + xx)

    def x_at(d):
        return (x + d) % nx, device((x + d) % nx, y, z, core)

    def y_at(d):
        return (y + d) % ny, device(x, (y + d) % ny, z, core)

    def z_at(d):
        return (z + d) % nz, device(x, y, (z + d) % nz, core)

    sibling = device(x, y, z, 1 - core)
    cross = [((z + d) % nz, device(x, y, (z + d) % nz, 1 - core)) for d in near_first(nz)]

    loads = {}
    for i, (name, src, dst) in enumerate([
        ("cot", cot_hbm, cot), ("own", feat_hbm, col_src_0.at[z, core]), ("rows", rows_hbm, rows),
        ("cols", cols_hbm, cols), ("count", count_hbm, count), ("w_in", w_in_hbm, w_in),
        ("w_hid", w_hid_hbm, w_hid), ("tiles", tiles_hbm, tiles),
    ]):
        loads[name] = pltpu.make_async_copy(src, dst, local_sem.at[i])
        loads[name].start()

    barrier = pltpu.get_barrier_semaphore()
    everyone = [x_at(d)[1] for d in near_first(nx)] + [y_at(d)[1] for d in near_first(ny)]
    everyone += [z_at(d)[1] for d in near_first(nz)] + [peer for _, peer in cross] + [sibling]
    for peer in everyone:
        pl.semaphore_signal(barrier, inc=1, device_id=peer, device_id_type=MESH)

    sends = []
    used = [0, 0]

    def new_recv(n=1):
        used[0] += n
        return used[0] - n

    def new_send(ref):
        sends.append((used[1], ref))
        used[1] += 1
        return used[1] - 1

    def push(src, dst, peer, s, r):
        pltpu.make_async_remote_copy(
            src_ref=src, dst_ref=dst, send_sem=ssem.at[s], recv_sem=rsem.at[r],
            device_id=peer, device_id_type=MESH,
        ).start()

    def landed(r, ref):
        pltpu.make_async_copy(ref, ref, rsem.at[r]).wait()

    def gather_col_start(rnd):
        buf = col_src[rnd]
        z_recv, c_recv = new_recv(nz), new_recv()
        s = new_send(buf.at[0 : nz - 1, 0])
        for d in near_first(nz):
            push(buf.at[z, core], buf.at[z, core], z_at(d)[1], s, z_recv + d)
        c_send = new_send(buf.at[:, 0])
        push(buf.at[z, core], buf.at[z, core], sibling, c_send, c_recv)
        return z_recv, c_recv, c_send

    def gather_col_pass(rnd, sems, d):
        buf = col_src[rnd]
        z_recv, c_recv, c_send = sems
        src = (z + nz - d) % nz
        landed(z_recv + d, buf.at[src, core])
        push(buf.at[src, core], buf.at[src, core], sibling, c_send, c_recv)

    def gather_col_finish(rnd, sems):
        landed(sems[1], col_src[rnd].at[:, 0])

    def gather_row_start():
        y_recv = new_recv(ny)
        s = new_send(row_src.at[0 : ny - 1, 0, low])
        for d in near_first(ny):
            push(row_src.at[y, x, low], row_src.at[y, x, low], y_at(d)[1], s, y_recv + d)
        x_recv = new_recv()
        s = new_send(row_src.at[0, 0 : nx - 1])
        for d in near_first(nx):
            push(row_src.at[y, x], row_src.at[y, x], x_at(d)[1], s, x_recv)
        return y_recv, x_recv, new_recv(), new_send(row_src.at[0 : ny - 1, 0 : nx - 1, low])

    def gather_row_high(sems):
        landed(sems[1], row_src.at[0, 0 : nx - 1])
        r = new_recv()
        s = new_send(row_src.at[0 : ny - 1, :, high])
        for d in near_first(ny):
            push(row_src.at[y, :, high], row_src.at[y, :, high], y_at(d)[1], s, r)
        return r

    def gather_row_pass(sems, d):
        y_recv, _, r, s = sems
        src = (y + ny - d) % ny
        landed(y_recv + d, row_src.at[src, x, low])
        for e in far_first(nx):
            push(row_src.at[src, x, low], row_src.at[src, x, low], x_at(e)[1], s, r)

    def gather_row_finish(sems, high_recv):
        landed(sems[2], row_src.at[0 : ny - 1, 0 : nx - 1, low])
        landed(high_recv, row_src.at[0 : ny - 1, :, high])

    unroll = 8

    def spread_forward(rnd):
        src = col_src[rnd]

        def some(turn, acc):
            for i in range(unroll):
                k = turn * unroll + i
                c = meta[1, k]
                d = jnp.dot(tiles[meta[0, k]], src[c // 2, c % 2], preferred_element_type=F32)
                acc = jnp.where(meta[2, k] > 0, d, acc + d)
                part[k] = acc.astype(BF)
            return acc

        lax.fori_loop(0, slots // unroll, some, jnp.zeros((height, height), F32))

        def place(b, _):
            send_f[rnd, b // nx, b % nx] = part[meta[3, b]]
            return 0

        lax.fori_loop(0, nx * ny, place, 0)

    def spread_backward():
        def some(turn, acc):
            for i in range(unroll):
                k = turn * unroll + i
                r = meta[5, k]
                d = jnp.dot(row_src[r // nx, r % nx], tiles[meta[4, k]], preferred_element_type=F32)
                acc = jnp.where(meta[6, k] > 0, d, acc + d)
                part[k] = acc.astype(BF)
            return acc

        lax.fori_loop(0, slots // unroll, some, jnp.zeros((height, height), F32))

        def place(b, _):
            send_b[b // 2, b % 2] = part[meta[7, b]]
            return 0

        lax.fori_loop(0, nz * 2, place, 0)

    y_turns = far_first(ny) + [0]

    def reduce_rows_start(rnd):
        buf = send_f.at[rnd]
        a_recv, b_recv = new_recv(ny), new_recv()
        a_send = new_send(rx_a.at[rnd, :, 0 : nx - 1])
        b_send = new_send(ry_b.at[rnd, 0 : ny - 1])
        for i, dy in enumerate(y_turns):
            for dx in far_first(nx):
                px, peer = x_at(dx)
                push(buf.at[(y + dy) % ny, px, low], rx_a.at[rnd, dy, x], peer, a_send, a_recv + dy)
            if i < ny - 1:
                py, peer = y_at(dy)
                push(buf.at[py, :, high], ry_b.at[rnd, y], peer, b_send, b_recv)
        ya_recv, ya_send = new_recv(), new_send(ry_a.at[rnd, 0 : ny - 1])
        return a_recv, b_recv, ya_recv, ya_send

    def reduce_rows_pass(rnd, sems, dy):
        a_recv, _, ya_recv, ya_send = sems
        landed(a_recv + dy, rx_a.at[rnd, dy, 0 : nx - 1])
        total = send_f[rnd, (y + dy) % ny, x, 0:CUT].astype(F32)
        for dx in near_first(nx):
            total += rx_a[rnd, dy, (x + dx) % nx].astype(F32)
        if dy == 0:
            mid_a[rnd, 0] = total
        else:
            mid = ry_a.at[rnd, ny + dy]
            mid[...] = total.astype(BF)
            push(mid, ry_a.at[rnd, y], y_at(dy)[1], ya_send, ya_recv)

    def reduce_rows_high(rnd, sems):
        landed(sems[1], ry_b.at[rnd, 0 : ny - 1])
        r, s = new_recv(), new_send(rx_b.at[rnd, 0 : nx - 1])
        for dx in far_first(nx) + [0]:
            px = (x + dx) % nx
            total = send_f[rnd, y, px, CUT:height].astype(F32)
            for dy in near_first(ny):
                total += ry_b[rnd, (y + dy) % ny, px].astype(F32)
            if dx == 0:
                mid_b[rnd, 0] = total
            else:
                mid = rx_b.at[rnd, nx + dx]
                mid[...] = total.astype(BF)
                push(mid, rx_b.at[rnd, x], x_at(dx)[1], s, r)
        return r

    def reduce_rows_finish(rnd, sems, high_recv):
        landed(high_recv, rx_b.at[rnd, 0 : nx - 1])
        bottom = mid_b[rnd, 0]
        for dx in near_first(nx):
            bottom += rx_b[rnd, (x + dx) % nx].astype(F32)
        landed(sems[2], ry_a.at[rnd, 0 : ny - 1])
        top = mid_a[rnd, 0]
        for dy in near_first(ny):
            top += ry_a[rnd, (y + dy) % ny].astype(F32)
        return jnp.concatenate([top, bottom], axis=0)

    def reduce_cols_start():
        r = new_recv()
        push(send_b.at[:, 1 - core], r_core, sibling, new_send(r_core), r)
        return r

    def reduce_cols_second(recv):
        landed(recv, r_core)
        r, s = new_recv(), new_send(r_z.at[0 : nz - 1])
        for d in near_first(nz):
            pz, peer = z_at(d)
            mid_z[pz] = (send_b[pz, core].astype(F32) + r_core[pz].astype(F32)).astype(BF)
            push(mid_z.at[pz], r_z.at[z], peer, s, r)
        return r

    def reduce_cols_finish(recv):
        total = send_b[z, core].astype(F32) + r_core[z].astype(F32)
        landed(recv, r_z.at[0 : nz - 1])
        for d in near_first(nz):
            total += r_z[(z + d) % nz].astype(F32)
        return total.astype(BF)

    part[slots] = jnp.zeros((height, height), BF)
    loads["cot"].wait()
    loads["own"].wait()
    row_src[y, x] = cot[...].astype(F32).T.astype(BF)
    pl.semaphore_wait(barrier, len(everyone))

    col_sems = gather_col_start(0)
    row_sems = gather_row_start()
    loads["rows"].wait()
    loads["cols"].wait()
    loads["count"].wait()
    live = count[0, 0]
    meta_v[...] = jnp.zeros_like(meta_v)
    for i, line in enumerate(slot_order(rows[0], cols[0], live, nx * ny) + slot_order(cols[0], rows[0], live, nz * 2)):
        meta_v[i : i + 1, 0:slots] = line
    meta_copy = pltpu.make_async_copy(meta_v, meta, local_sem.at[8])
    meta_copy.start()
    high_recv = gather_row_high(row_sems)
    for i in range(1, max(ny, nz)):
        if i < nz:
            gather_col_pass(0, col_sems, near_first(nz)[i - 1])
        if i < ny:
            gather_row_pass(row_sems, near_first(ny)[i - 1])
    meta_copy.wait()
    loads["tiles"].wait()
    gather_col_finish(0, col_sems)
    spread_forward(0)
    sum_sems = reduce_rows_start(0)
    for dy in y_turns[0:2]:
        reduce_rows_pass(0, sum_sems, dy)
    gather_row_finish(row_sems, high_recv)
    spread_backward()
    core_recv = reduce_cols_start()
    for dy in y_turns[2:4]:
        reduce_rows_pass(0, sum_sems, dy)
    z_recv = reduce_cols_second(core_recv)
    for dy in y_turns[4:]:
        reduce_rows_pass(0, sum_sems, dy)
    high_recv = reduce_rows_high(0, sum_sems)
    loads["w_in"].wait()
    loads["w_hid"].wait()
    mixed = reduce_rows_finish(0, sum_sems, high_recv)
    sum_first = split_dot(mixed, w_in[...])
    col_src_1[z, core] = (sum_first / (1.0 + jnp.exp(-sum_first))).astype(BF)

    col_sems = gather_col_start(1)
    mixed_t = mixed.T.astype(BF)
    sum_t = sum_first.T
    gate_t = 1.0 / (1.0 + jnp.exp(-sum_t))
    hidden_t = (sum_t * gate_t).astype(BF)
    slope_t = gate_t * (1.0 + sum_t * (1.0 - gate_t))
    grad_t = reduce_cols_finish(z_recv)
    grad_sum_t = (jnp.dot(w_hid[...], grad_t, preferred_element_type=F32) * slope_t).astype(BF)
    term[0:height] = lax.dot_general(mixed_t, grad_sum_t, CONTRACT_LAST, preferred_element_type=F32).astype(BF)
    term[height : 2 * height] = lax.dot_general(
        hidden_t, grad_t, CONTRACT_LAST, preferred_element_type=F32
    ).astype(BF)
    band = height // nz
    row_peers = [(z_at(d)[0] * 2 + core, z_at(d)[1]) for d in near_first(nz)]
    row_peers += [(pz * 2 + 1 - core, peer) for pz, peer in cross]
    row_peers += [(z * 2 + 1 - core, sibling)]

    def rows_of(i):
        return pl.ds(pl.multiple_of(i * band, band), band)

    r_row, s_row = new_recv(), new_send(ar_row.at[0 : 2 * nz - 1])
    for i, peer in row_peers:
        push(term.at[rows_of(i)], ar_row.at[row], peer, s_row, r_row)
    for d in near_first(nz):
        gather_col_pass(1, col_sems, d)
    landed(r_row, ar_row.at[0 : 2 * nz - 1])
    total = term[rows_of(row)].astype(F32)
    for i, _ in row_peers:
        total += ar_row[i].astype(F32)
    ar_x[x] = total.astype(BF)
    r_x, s_x = new_recv(), new_send(ar_x.at[0 : nx - 1])
    for d in far_first(nx):
        push(ar_x.at[x], ar_x.at[x], x_at(d)[1], s_x, r_x)
    gather_col_finish(1, col_sems)
    spread_forward(1)
    sum_sems = reduce_rows_start(1)
    landed(r_x, ar_x.at[0 : nx - 1])
    total = ar_x[0].astype(F32)
    for i in range(1, nx):
        total += ar_x[i].astype(F32)
    ar_y[y] = total.astype(BF)
    r_y, s_y = new_recv(), new_send(ar_y.at[0 : ny - 1])
    for d in far_first(ny):
        push(ar_y.at[y], ar_y.at[y], y_at(d)[1], s_y, r_y)
    for dy in y_turns[0:4]:
        reduce_rows_pass(1, sum_sems, dy)
    landed(r_y, ar_y.at[0 : ny - 1])
    total = ar_y[0].astype(F32)
    for i in range(1, ny):
        total += ar_y[i].astype(F32)
    ar_out[rows_of(row)] = total.astype(BF)
    r_out, s_out = new_recv(), new_send(ar_out.at[0 : 2 * height - band])
    for _, peer in row_peers:
        push(ar_out.at[rows_of(row)], ar_out.at[rows_of(row)], peer, s_out, r_out)
    for dy in y_turns[4:]:
        reduce_rows_pass(1, sum_sems, dy)
    high_recv = reduce_rows_high(1, sum_sems)
    landed(r_out, ar_out.at[0 : 2 * height - band])
    gw_in[...] = ar_out[0:height].astype(F32)
    gw_hid[...] = ar_out[height : 2 * height].astype(F32)
    logits[...] = split_dot(reduce_rows_finish(1, sum_sems, high_recv), w_hid[...])

    for s, ref in sends:
        pltpu.make_async_copy(ref, ref, ssem.at[s]).wait()


def write_out(a, b, c, a_out, b_out, c_out, sem):
    copies = [pltpu.make_async_copy(s, d, sem.at[i]) for i, (s, d) in enumerate([(a, a_out), (b, b_out), (c, c_out)])]
    for copy in copies:
        copy.start()
    for copy in copies:
        copy.wait()


def body(nx, features, weight_in, weight_hidden, tile_rows, tile_cols, tile_values, tile_counts, cotangent):
    nz = lax.axis_size("row") // 2
    ny = lax.axis_size(("col", "rep")) // nx
    slots, height = tile_values.shape[2], tile_values.shape[3]
    rest = height - CUT
    band = height // nz
    block = (height, height)
    vmem = pl.BlockSpec(memory_space=pltpu.VMEM)
    hbm = pl.BlockSpec(memory_space=pltpu.HBM)
    results = [jax.ShapeDtypeStruct(block, F32)] * 3
    outs = pl.pallas_call(
        functools.partial(kernel, nx, ny, nz, slots),
        out_shape=results,
        in_specs=[hbm] * 8,
        out_specs=[vmem] * 3,
        scratch_shapes=[
            pltpu.VMEM(block, BF),
            pltpu.VMEM(block, BF),
            pltpu.VMEM((1, 1, slots), I32),
            pltpu.VMEM((1, 1, slots), I32),
            pltpu.VMEM((slots,) + block, BF),
            pltpu.SMEM((1, 1), I32),
            pltpu.VMEM(block, BF),
            pltpu.VMEM((8, 128), I32),
            pltpu.SMEM((8, 128), I32),
            pltpu.VMEM((nz, 2) + block, BF),
            pltpu.VMEM((nz, 2) + block, BF),
            pltpu.VMEM((ny, nx) + block, BF),
            pltpu.VMEM((slots + 1,) + block, BF),
            pltpu.VMEM((2, ny, nx) + block, BF),
            pltpu.VMEM((2, ny, nx, CUT, height), BF),
            pltpu.VMEM((2, 2 * nx, rest, height), BF),
            pltpu.VMEM((2, 1, CUT, height), F32),
            pltpu.VMEM((2, 1, rest, height), F32),
            pltpu.VMEM((2, 2 * ny, CUT, height), BF),
            pltpu.VMEM((2, ny, nx, rest, height), BF),
            pltpu.VMEM((nz, 2) + block, BF),
            pltpu.VMEM((nz,) + block, BF),
            pltpu.VMEM((nz,) + block, BF),
            pltpu.VMEM((nz,) + block, BF),
            pltpu.VMEM((2 * height, height), BF),
            pltpu.VMEM((2 * nz, band, height), BF),
            pltpu.VMEM((nx, band, height), BF),
            pltpu.VMEM((ny, band, height), BF),
            pltpu.VMEM((2 * height, height), BF),
            pltpu.SemaphoreType.DMA((9,)),
            pltpu.SemaphoreType.DMA((40,)),
            pltpu.SemaphoreType.DMA((72,)),
        ],
        compiler_params=pltpu.CompilerParams(
            collective_id=0, has_side_effects=True, vmem_limit_bytes=56 * 1024 * 1024
        ),
    )(
        features, weight_in, weight_hidden, tile_rows, tile_cols,
        tile_values.reshape((slots,) + block), tile_counts, cotangent,
    )
    return pl.pallas_call(
        write_out,
        out_shape=results,
        in_specs=[vmem] * 3,
        out_specs=[hbm] * 3,
        scratch_shapes=[pltpu.SemaphoreType.DMA((3,))],
    )(*outs)


def solution(mesh, nx=4):
    return jax.shard_map(
        functools.partial(body, nx),
        mesh=mesh,
        in_specs=(
            P(("row", "col", "rep"), None),
            P(),
            P(),
            P("row", ("col", "rep"), None),
            P("row", ("col", "rep"), None),
            P("row", ("col", "rep"), None, None, None),
            P("row", ("col", "rep")),
            P(("row", "col", "rep"), None),
        ),
        out_specs=(P(("row", "col", "rep"), None), P(), P()),
        check_vma=False,
    )
```

```python
import functools

import jax
import jax.numpy as jnp
from jax import lax
from jax.experimental import pallas as pl
from jax.experimental.pallas import tpu as pltpu
from jax.sharding import PartitionSpec as P

MESH = pl.DeviceIdType.MESH
BF = jnp.bfloat16
F32 = jnp.float32
I32 = jnp.int32
CONTRACT_LAST = (((1,), (1,)), ((), ()))
CUT = 96


def near_first(n):
    return sorted(range(1, n), key=lambda d: (min(d, n - d), d))


def far_first(n):
    return near_first(n)[::-1]


def split_dot(wide, weight):
    head = wide.astype(BF)
    rest = (wide - head.astype(F32)).astype(BF)
    return jnp.dot(head, weight, preferred_element_type=F32) + jnp.dot(rest, weight, preferred_element_type=F32)


def slot_order(group, other, count, groups):
    slots = group.shape[1]
    down = lax.broadcasted_iota(I32, (slots, slots), 0)
    along = lax.broadcasted_iota(I32, (slots, slots), 1)
    live = along < count

    def upright(row):
        return jnp.sum(jnp.where(down == along, row, 0), axis=1, keepdims=True)

    key = jnp.where(live, jnp.broadcast_to(group, (slots, slots)), groups)
    key_down = upright(key)
    other_down = upright(jnp.where(live, jnp.broadcast_to(other, (slots, slots)), 0))
    ahead = jnp.where((key == key_down) & (along < down), 1, 0)
    rank = jnp.sum(jnp.where(key < key_down, 1, ahead), axis=1, keepdims=True)
    opens = jnp.where(jnp.sum(ahead, axis=1, keepdims=True) == 0, 1, 0)
    here = rank == along

    def placed(value):
        return jnp.sum(jnp.where(here, value, 0), axis=0, keepdims=True)

    upto = jnp.sum(jnp.where(key_down <= along, 1, 0), axis=0, keepdims=True)
    found = jnp.sum(jnp.where(key_down == along, 1, 0), axis=0, keepdims=True)
    last = jnp.where(found > 0, upto - 1, slots)
    return placed(down), placed(other_down), placed(opens), last


def kernel(
    nx, ny, nz, slots,
    feat_hbm, w_in_hbm, w_hid_hbm, rows_hbm, cols_hbm, tiles_hbm, count_hbm, cot_hbm,
    logits, gw_in, gw_hid,
    w_in, w_hid, rows, cols, tiles, count, cot, meta_v, meta,
    col_src_0, col_src_1, row_src, part, send_f, rx_a, rx_b, mid_a, mid_b, ry_a, ry_b,
    send_b, r_core, mid_z, r_z, term, ar_row, ar_x, ar_y, ar_out,
    local_sem, ssem, rsem,
):
    row = lax.axis_index("row")
    col = lax.axis_index("col")
    rep = lax.axis_index("rep")
    reps_y = lax.axis_size("rep") // nx
    z, core = row // 2, row % 2
    y, x = col * reps_y + rep // nx, rep % nx
    height = cot.shape[0]
    low, high = pl.ds(0, CUT), pl.ds(CUT, height - CUT)
    col_src = (col_src_0, col_src_1)

    def device(xx, yy, zz, cc):
        return (zz * 2 + cc, yy // reps_y, (yy % reps_y) * nx + xx)

    def x_at(d):
        return (x + d) % nx, device((x + d) % nx, y, z, core)

    def y_at(d):
        return (y + d) % ny, device(x, (y + d) % ny, z, core)

    def z_at(d):
        return (z + d) % nz, device(x, y, (z + d) % nz, core)

    sibling = device(x, y, z, 1 - core)
    cross = [((z + d) % nz, device(x, y, (z + d) % nz, 1 - core)) for d in near_first(nz)]

    loads = {}
    for i, (name, src, dst) in enumerate([
        ("cot", cot_hbm, cot), ("own", feat_hbm, col_src_0.at[z, core]), ("rows", rows_hbm, rows),
        ("cols", cols_hbm, cols), ("count", count_hbm, count), ("w_in", w_in_hbm, w_in),
        ("w_hid", w_hid_hbm, w_hid), ("tiles", tiles_hbm, tiles),
    ]):
        loads[name] = pltpu.make_async_copy(src, dst, local_sem.at[i])
        loads[name].start()

    barrier = pltpu.get_barrier_semaphore()
    everyone = [x_at(d)[1] for d in near_first(nx)] + [y_at(d)[1] for d in near_first(ny)]
    everyone += [z_at(d)[1] for d in near_first(nz)] + [peer for _, peer in cross] + [sibling]
    for peer in everyone:
        pl.semaphore_signal(barrier, inc=1, device_id=peer, device_id_type=MESH)

    sends = []
    used = [0, 0]

    def new_recv(n=1):
        used[0] += n
        return used[0] - n

    def new_send(ref):
        sends.append((used[1], ref))
        used[1] += 1
        return used[1] - 1

    def push(src, dst, peer, s, r):
        pltpu.make_async_remote_copy(
            src_ref=src, dst_ref=dst, send_sem=ssem.at[s], recv_sem=rsem.at[r],
            device_id=peer, device_id_type=MESH,
        ).start()

    def landed(r, ref):
        pltpu.make_async_copy(ref, ref, rsem.at[r]).wait()

    def gather_col_start(rnd):
        buf = col_src[rnd]
        z_recv, c_recv = new_recv(nz), new_recv()
        s = new_send(buf.at[0 : nz - 1, 0])
        for d in near_first(nz):
            push(buf.at[z, core], buf.at[z, core], z_at(d)[1], s, z_recv + d)
        c_send = new_send(buf.at[:, 0])
        push(buf.at[z, core], buf.at[z, core], sibling, c_send, c_recv)
        return z_recv, c_recv, c_send

    def gather_col_pass(rnd, sems, d):
        buf = col_src[rnd]
        z_recv, c_recv, c_send = sems
        src = (z + nz - d) % nz
        landed(z_recv + d, buf.at[src, core])
        push(buf.at[src, core], buf.at[src, core], sibling, c_send, c_recv)

    def gather_col_finish(rnd, sems):
        landed(sems[1], col_src[rnd].at[:, 0])

    def gather_row_start():
        y_recv = new_recv(ny)
        s = new_send(row_src.at[0 : ny - 1, 0, low])
        for d in near_first(ny):
            push(row_src.at[y, x, low], row_src.at[y, x, low], y_at(d)[1], s, y_recv + d)
        x_recv = new_recv()
        s = new_send(row_src.at[0, 0 : nx - 1])
        for d in near_first(nx):
            push(row_src.at[y, x], row_src.at[y, x], x_at(d)[1], s, x_recv)
        return y_recv, x_recv, new_recv(), new_send(row_src.at[0 : ny - 1, 0 : nx - 1, low])

    def gather_row_high(sems):
        landed(sems[1], row_src.at[0, 0 : nx - 1])
        r = new_recv()
        s = new_send(row_src.at[0 : ny - 1, :, high])
        for d in near_first(ny):
            push(row_src.at[y, :, high], row_src.at[y, :, high], y_at(d)[1], s, r)
        return r

    def gather_row_pass(sems, d):
        y_recv, _, r, s = sems
        src = (y + ny - d) % ny
        landed(y_recv + d, row_src.at[src, x, low])
        for e in far_first(nx):
            push(row_src.at[src, x, low], row_src.at[src, x, low], x_at(e)[1], s, r)

    def gather_row_finish(sems, high_recv):
        landed(sems[2], row_src.at[0 : ny - 1, 0 : nx - 1, low])
        landed(high_recv, row_src.at[0 : ny - 1, :, high])

    unroll = 32

    def spread_forward(rnd):
        src = col_src[rnd]

        def some(turn, acc):
            for i in range(unroll):
                k = turn * unroll + i
                c = meta[1, k]
                d = jnp.dot(tiles[meta[0, k]], src[c // 2, c % 2], preferred_element_type=F32)
                acc = jnp.where(meta[2, k] > 0, d, acc + d)
                part[k] = acc.astype(BF)
            return acc

        lax.fori_loop(0, slots // unroll, some, jnp.zeros((height, height), F32))

        def place(b, _):
            send_f[rnd, b // nx, b % nx] = part[meta[3, b]]
            return 0

        lax.fori_loop(0, nx * ny, place, 0)

    def spread_backward():
        def some(turn, acc):
            for i in range(unroll):
                k = turn * unroll + i
                r = meta[5, k]
                d = jnp.dot(row_src[r // nx, r % nx], tiles[meta[4, k]], preferred_element_type=F32)
                acc = jnp.where(meta[6, k] > 0, d, acc + d)
                part[k] = acc.astype(BF)
            return acc

        lax.fori_loop(0, slots // unroll, some, jnp.zeros((height, height), F32))

        def place(b, _):
            send_b[b // 2, b % 2] = part[meta[7, b]]
            return 0

        lax.fori_loop(0, nz * 2, place, 0)

    y_turns = far_first(ny) + [0]

    def reduce_rows_start(rnd):
        buf = send_f.at[rnd]
        a_recv, b_recv = new_recv(ny), new_recv()
        a_send = new_send(rx_a.at[rnd, :, 0 : nx - 1])
        b_send = new_send(ry_b.at[rnd, 0 : ny - 1])
        for i, dy in enumerate(y_turns):
            for dx in far_first(nx):
                px, peer = x_at(dx)
                push(buf.at[(y + dy) % ny, px, low], rx_a.at[rnd, dy, x], peer, a_send, a_recv + dy)
            if i < ny - 1:
                py, peer = y_at(dy)
                push(buf.at[py, :, high], ry_b.at[rnd, y], peer, b_send, b_recv)
        ya_recv, ya_send = new_recv(), new_send(ry_a.at[rnd, 0 : ny - 1])
        return a_recv, b_recv, ya_recv, ya_send

    def reduce_rows_pass(rnd, sems, dy):
        a_recv, _, ya_recv, ya_send = sems
        landed(a_recv + dy, rx_a.at[rnd, dy, 0 : nx - 1])
        total = send_f[rnd, (y + dy) % ny, x, 0:CUT].astype(F32)
        for dx in near_first(nx):
            total += rx_a[rnd, dy, (x + dx) % nx].astype(F32)
        if dy == 0:
            mid_a[rnd, 0] = total
        else:
            mid = ry_a.at[rnd, ny + dy]
            mid[...] = total.astype(BF)
            push(mid, ry_a.at[rnd, y], y_at(dy)[1], ya_send, ya_recv)

    def reduce_rows_high(rnd, sems):
        landed(sems[1], ry_b.at[rnd, 0 : ny - 1])
        r, s = new_recv(), new_send(rx_b.at[rnd, 0 : nx - 1])
        for dx in far_first(nx) + [0]:
            px = (x + dx) % nx
            total = send_f[rnd, y, px, CUT:height].astype(F32)
            for dy in near_first(ny):
                total += ry_b[rnd, (y + dy) % ny, px].astype(F32)
            if dx == 0:
                mid_b[rnd, 0] = total
            else:
                mid = rx_b.at[rnd, nx + dx]
                mid[...] = total.astype(BF)
                push(mid, rx_b.at[rnd, x], x_at(dx)[1], s, r)
        return r

    def reduce_rows_finish(rnd, sems, high_recv):
        landed(high_recv, rx_b.at[rnd, 0 : nx - 1])
        bottom = mid_b[rnd, 0]
        for dx in near_first(nx):
            bottom += rx_b[rnd, (x + dx) % nx].astype(F32)
        landed(sems[2], ry_a.at[rnd, 0 : ny - 1])
        top = mid_a[rnd, 0]
        for dy in near_first(ny):
            top += ry_a[rnd, (y + dy) % ny].astype(F32)
        return jnp.concatenate([top, bottom], axis=0)

    def reduce_cols_start():
        r = new_recv()
        push(send_b.at[:, 1 - core], r_core, sibling, new_send(r_core), r)
        return r

    def reduce_cols_second(recv):
        landed(recv, r_core)
        r, s = new_recv(), new_send(r_z.at[0 : nz - 1])
        for d in near_first(nz):
            pz, peer = z_at(d)
            mid_z[pz] = (send_b[pz, core].astype(F32) + r_core[pz].astype(F32)).astype(BF)
            push(mid_z.at[pz], r_z.at[z], peer, s, r)
        return r

    def reduce_cols_finish(recv):
        total = send_b[z, core].astype(F32) + r_core[z].astype(F32)
        landed(recv, r_z.at[0 : nz - 1])
        for d in near_first(nz):
            total += r_z[(z + d) % nz].astype(F32)
        return total.astype(BF)

    part[slots] = jnp.zeros((height, height), BF)
    loads["cot"].wait()
    loads["own"].wait()
    row_src[y, x] = cot[...].astype(F32).T.astype(BF)
    pl.semaphore_wait(barrier, len(everyone))

    col_sems = gather_col_start(0)
    row_sems = gather_row_start()
    loads["rows"].wait()
    loads["cols"].wait()
    loads["count"].wait()
    live = count[0, 0]
    meta_v[...] = jnp.zeros_like(meta_v)
    for i, line in enumerate(slot_order(rows[0], cols[0], live, nx * ny) + slot_order(cols[0], rows[0], live, nz * 2)):
        meta_v[i : i + 1, 0:slots] = line
    meta_copy = pltpu.make_async_copy(meta_v, meta, local_sem.at[8])
    meta_copy.start()
    high_recv = gather_row_high(row_sems)
    for i in range(1, max(ny, nz)):
        if i < nz:
            gather_col_pass(0, col_sems, near_first(nz)[i - 1])
        if i < ny:
            gather_row_pass(row_sems, near_first(ny)[i - 1])
    meta_copy.wait()
    loads["tiles"].wait()
    gather_col_finish(0, col_sems)
    spread_forward(0)
    sum_sems = reduce_rows_start(0)
    gather_row_finish(row_sems, high_recv)
    spread_backward()
    core_recv = reduce_cols_start()
    for dy in y_turns[0:2]:
        reduce_rows_pass(0, sum_sems, dy)
    z_recv = reduce_cols_second(core_recv)
    for dy in y_turns[2:]:
        reduce_rows_pass(0, sum_sems, dy)
    high_recv = reduce_rows_high(0, sum_sems)
    loads["w_in"].wait()
    loads["w_hid"].wait()
    mixed = reduce_rows_finish(0, sum_sems, high_recv)
    sum_first = split_dot(mixed, w_in[...])
    col_src_1[z, core] = (sum_first / (1.0 + jnp.exp(-sum_first))).astype(BF)

    col_sems = gather_col_start(1)
    mixed_t = mixed.T.astype(BF)
    sum_t = sum_first.T
    gate_t = 1.0 / (1.0 + jnp.exp(-sum_t))
    hidden_t = (sum_t * gate_t).astype(BF)
    slope_t = gate_t * (1.0 + sum_t * (1.0 - gate_t))
    grad_t = reduce_cols_finish(z_recv)
    grad_sum_t = (jnp.dot(w_hid[...], grad_t, preferred_element_type=F32) * slope_t).astype(BF)
    term[0:height] = lax.dot_general(mixed_t, grad_sum_t, CONTRACT_LAST, preferred_element_type=F32).astype(BF)
    term[height : 2 * height] = lax.dot_general(
        hidden_t, grad_t, CONTRACT_LAST, preferred_element_type=F32
    ).astype(BF)
    band = height // nz
    row_peers = [(z_at(d)[0] * 2 + core, z_at(d)[1]) for d in near_first(nz)]
    row_peers += [(pz * 2 + 1 - core, peer) for pz, peer in cross]
    row_peers += [(z * 2 + 1 - core, sibling)]

    def rows_of(i):
        return pl.ds(pl.multiple_of(i * band, band), band)

    r_row, s_row = new_recv(), new_send(ar_row.at[0 : 2 * nz - 1])
    for i, peer in row_peers:
        push(term.at[rows_of(i)], ar_row.at[row], peer, s_row, r_row)
    for d in near_first(nz):
        gather_col_pass(1, col_sems, d)
    landed(r_row, ar_row.at[0 : 2 * nz - 1])
    total = term[rows_of(row)].astype(F32)
    for i, _ in row_peers:
        total += ar_row[i].astype(F32)
    ar_x[x] = total.astype(BF)
    r_x, s_x = new_recv(), new_send(ar_x.at[0 : nx - 1])
    for d in far_first(nx):
        push(ar_x.at[x], ar_x.at[x], x_at(d)[1], s_x, r_x)
    gather_col_finish(1, col_sems)
    spread_forward(1)
    sum_sems = reduce_rows_start(1)
    landed(r_x, ar_x.at[0 : nx - 1])
    total = ar_x[0].astype(F32)
    for i in range(1, nx):
        total += ar_x[i].astype(F32)
    ar_y[y] = total.astype(BF)
    r_y, s_y = new_recv(), new_send(ar_y.at[0 : ny - 1])
    for d in far_first(ny):
        push(ar_y.at[y], ar_y.at[y], y_at(d)[1], s_y, r_y)
    for dy in y_turns[0:4]:
        reduce_rows_pass(1, sum_sems, dy)
    landed(r_y, ar_y.at[0 : ny - 1])
    total = ar_y[0].astype(F32)
    for i in range(1, ny):
        total += ar_y[i].astype(F32)
    ar_out[rows_of(row)] = total.astype(BF)
    r_out, s_out = new_recv(), new_send(ar_out.at[0 : 2 * height - band])
    for _, peer in row_peers:
        push(ar_out.at[rows_of(row)], ar_out.at[rows_of(row)], peer, s_out, r_out)
    for dy in y_turns[4:]:
        reduce_rows_pass(1, sum_sems, dy)
    high_recv = reduce_rows_high(1, sum_sems)
    landed(r_out, ar_out.at[0 : 2 * height - band])
    gw_in[...] = ar_out[0:height].astype(F32)
    gw_hid[...] = ar_out[height : 2 * height].astype(F32)
    logits[...] = split_dot(reduce_rows_finish(1, sum_sems, high_recv), w_hid[...])

    for s, ref in sends:
        pltpu.make_async_copy(ref, ref, ssem.at[s]).wait()


def write_out(a, b, c, a_out, b_out, c_out, sem):
    copies = [pltpu.make_async_copy(s, d, sem.at[i]) for i, (s, d) in enumerate([(a, a_out), (b, b_out), (c, c_out)])]
    for copy in copies:
        copy.start()
    for copy in copies:
        copy.wait()


def body(nx, features, weight_in, weight_hidden, tile_rows, tile_cols, tile_values, tile_counts, cotangent):
    nz = lax.axis_size("row") // 2
    ny = lax.axis_size(("col", "rep")) // nx
    slots, height = tile_values.shape[2], tile_values.shape[3]
    rest = height - CUT
    band = height // nz
    block = (height, height)
    vmem = pl.BlockSpec(memory_space=pltpu.VMEM)
    hbm = pl.BlockSpec(memory_space=pltpu.HBM)
    results = [jax.ShapeDtypeStruct(block, F32)] * 3
    outs = pl.pallas_call(
        functools.partial(kernel, nx, ny, nz, slots),
        out_shape=results,
        in_specs=[hbm] * 8,
        out_specs=[vmem] * 3,
        scratch_shapes=[
            pltpu.VMEM(block, BF),
            pltpu.VMEM(block, BF),
            pltpu.VMEM((1, 1, slots), I32),
            pltpu.VMEM((1, 1, slots), I32),
            pltpu.VMEM((slots,) + block, BF),
            pltpu.SMEM((1, 1), I32),
            pltpu.VMEM(block, BF),
            pltpu.VMEM((8, 128), I32),
            pltpu.SMEM((8, 128), I32),
            pltpu.VMEM((nz, 2) + block, BF),
            pltpu.VMEM((nz, 2) + block, BF),
            pltpu.VMEM((ny, nx) + block, BF),
            pltpu.VMEM((slots + 1,) + block, BF),
            pltpu.VMEM((2, ny, nx) + block, BF),
            pltpu.VMEM((2, ny, nx, CUT, height), BF),
            pltpu.VMEM((2, 2 * nx, rest, height), BF),
            pltpu.VMEM((2, 1, CUT, height), F32),
            pltpu.VMEM((2, 1, rest, height), F32),
            pltpu.VMEM((2, 2 * ny, CUT, height), BF),
            pltpu.VMEM((2, ny, nx, rest, height), BF),
            pltpu.VMEM((nz, 2) + block, BF),
            pltpu.VMEM((nz,) + block, BF),
            pltpu.VMEM((nz,) + block, BF),
            pltpu.VMEM((nz,) + block, BF),
            pltpu.VMEM((2 * height, height), BF),
            pltpu.VMEM((2 * nz, band, height), BF),
            pltpu.VMEM((nx, band, height), BF),
            pltpu.VMEM((ny, band, height), BF),
            pltpu.VMEM((2 * height, height), BF),
            pltpu.SemaphoreType.DMA((9,)),
            pltpu.SemaphoreType.DMA((40,)),
            pltpu.SemaphoreType.DMA((72,)),
        ],
        compiler_params=pltpu.CompilerParams(
            collective_id=0, has_side_effects=True, vmem_limit_bytes=56 * 1024 * 1024
        ),
    )(
        features, weight_in, weight_hidden, tile_rows, tile_cols,
        tile_values.reshape((slots,) + block), tile_counts, cotangent,
    )
    return pl.pallas_call(
        write_out,
        out_shape=results,
        in_specs=[vmem] * 3,
        out_specs=[hbm] * 3,
        scratch_shapes=[pltpu.SemaphoreType.DMA((3,))],
    )(*outs)


def solution(mesh, nx=4):
    return jax.shard_map(
        functools.partial(body, nx),
        mesh=mesh,
        in_specs=(
            P(("row", "col", "rep"), None),
            P(),
            P(),
            P("row", ("col", "rep"), None),
            P("row", ("col", "rep"), None),
            P("row", ("col", "rep"), None, None, None),
            P("row", ("col", "rep")),
            P(("row", "col", "rep"), None),
        ),
        out_specs=(P(("row", "col", "rep"), None), P(), P()),
        check_vma=False,
    )
```

```python
import functools

import jax
import jax.numpy as jnp
from jax import lax
from jax.experimental import pallas as pl
from jax.experimental.pallas import tpu as pltpu
from jax.sharding import PartitionSpec as P

MESH = pl.DeviceIdType.MESH
BF = jnp.bfloat16
F32 = jnp.float32
I32 = jnp.int32
CONTRACT_LAST = (((1,), (1,)), ((), ()))
CUT = 96


def near_first(n):
    return sorted(range(1, n), key=lambda d: (min(d, n - d), d))


def far_first(n):
    return near_first(n)[::-1]


def split_dot(wide, weight):
    head = wide.astype(BF)
    rest = (wide - head.astype(F32)).astype(BF)
    return jnp.dot(head, weight, preferred_element_type=F32) + jnp.dot(rest, weight, preferred_element_type=F32)


def slot_order(group, other, count, groups):
    slots = group.shape[1]
    down = lax.broadcasted_iota(I32, (slots, slots), 0)
    along = lax.broadcasted_iota(I32, (slots, slots), 1)
    live = along < count

    def upright(row):
        return jnp.sum(jnp.where(down == along, row, 0), axis=1, keepdims=True)

    key = jnp.where(live, jnp.broadcast_to(group, (slots, slots)), groups)
    key_down = upright(key)
    other_down = upright(jnp.where(live, jnp.broadcast_to(other, (slots, slots)), 0))
    ahead = jnp.where((key == key_down) & (along < down), 1, 0)
    rank = jnp.sum(jnp.where(key < key_down, 1, ahead), axis=1, keepdims=True)
    opens = jnp.where(jnp.sum(ahead, axis=1, keepdims=True) == 0, 1, 0)
    here = rank == along

    def placed(value):
        return jnp.sum(jnp.where(here, value, 0), axis=0, keepdims=True)

    upto = jnp.sum(jnp.where(key_down <= along, 1, 0), axis=0, keepdims=True)
    found = jnp.sum(jnp.where(key_down == along, 1, 0), axis=0, keepdims=True)
    last = jnp.where(found > 0, upto - 1, slots)
    return placed(down), placed(other_down), placed(opens), last


def kernel(
    nx, ny, nz, slots,
    feat_hbm, w_in_hbm, w_hid_hbm, rows_hbm, cols_hbm, tiles_hbm, count_hbm, cot_hbm,
    logits, gw_in, gw_hid,
    w_in, w_hid, rows, cols, tiles, count, cot, meta_v, meta,
    col_src_0, col_src_1, row_src, part, send_f, rx_a, rx_b, mid_a, mid_b, ry_a, ry_b,
    send_b, r_core, mid_z, r_z, term, ar_x, ar_y, ar_core, ar_z, ar_out,
    local_sem, ssem, rsem,
):
    row = lax.axis_index("row")
    col = lax.axis_index("col")
    rep = lax.axis_index("rep")
    reps_y = lax.axis_size("rep") // nx
    z, core = row // 2, row % 2
    y, x = col * reps_y + rep // nx, rep % nx
    height = cot.shape[0]
    low, high = pl.ds(0, CUT), pl.ds(CUT, height - CUT)
    col_src = (col_src_0, col_src_1)

    def device(xx, yy, zz, cc):
        return (zz * 2 + cc, yy // reps_y, (yy % reps_y) * nx + xx)

    def x_at(d):
        return (x + d) % nx, device((x + d) % nx, y, z, core)

    def y_at(d):
        return (y + d) % ny, device(x, (y + d) % ny, z, core)

    def z_at(d):
        return (z + d) % nz, device(x, y, (z + d) % nz, core)

    sibling = device(x, y, z, 1 - core)

    loads = {}
    for i, (name, src, dst) in enumerate([
        ("cot", cot_hbm, cot), ("own", feat_hbm, col_src_0.at[z, core]), ("rows", rows_hbm, rows),
        ("cols", cols_hbm, cols), ("count", count_hbm, count), ("w_in", w_in_hbm, w_in),
        ("w_hid", w_hid_hbm, w_hid), ("tiles", tiles_hbm, tiles),
    ]):
        loads[name] = pltpu.make_async_copy(src, dst, local_sem.at[i])
        loads[name].start()

    barrier = pltpu.get_barrier_semaphore()
    everyone = [x_at(d)[1] for d in near_first(nx)] + [y_at(d)[1] for d in near_first(ny)]
    everyone += [z_at(d)[1] for d in near_first(nz)] + [sibling]
    for peer in everyone:
        pl.semaphore_signal(barrier, inc=1, device_id=peer, device_id_type=MESH)

    sends = []
    used = [0, 0]

    def new_recv(n=1):
        used[0] += n
        return used[0] - n

    def new_send(ref):
        sends.append((used[1], ref))
        used[1] += 1
        return used[1] - 1

    def push(src, dst, peer, s, r):
        pltpu.make_async_remote_copy(
            src_ref=src, dst_ref=dst, send_sem=ssem.at[s], recv_sem=rsem.at[r],
            device_id=peer, device_id_type=MESH,
        ).start()

    def landed(r, ref):
        pltpu.make_async_copy(ref, ref, rsem.at[r]).wait()

    def gather_col_start(rnd):
        buf = col_src[rnd]
        z_recv, c_recv = new_recv(nz), new_recv()
        s = new_send(buf.at[0 : nz - 1, 0])
        for d in near_first(nz):
            push(buf.at[z, core], buf.at[z, core], z_at(d)[1], s, z_recv + d)
        c_send = new_send(buf.at[:, 0])
        push(buf.at[z, core], buf.at[z, core], sibling, c_send, c_recv)
        return z_recv, c_recv, c_send

    def gather_col_pass(rnd, sems, d):
        buf = col_src[rnd]
        z_recv, c_recv, c_send = sems
        src = (z + nz - d) % nz
        landed(z_recv + d, buf.at[src, core])
        push(buf.at[src, core], buf.at[src, core], sibling, c_send, c_recv)

    def gather_col_finish(rnd, sems):
        landed(sems[1], col_src[rnd].at[:, 0])

    def gather_row_start():
        y_recv = new_recv(ny)
        s = new_send(row_src.at[0 : ny - 1, 0, low])
        for d in near_first(ny):
            push(row_src.at[y, x, low], row_src.at[y, x, low], y_at(d)[1], s, y_recv + d)
        x_recv = new_recv()
        s = new_send(row_src.at[0, 0 : nx - 1])
        for d in near_first(nx):
            push(row_src.at[y, x], row_src.at[y, x], x_at(d)[1], s, x_recv)
        return y_recv, x_recv, new_recv(), new_send(row_src.at[0 : ny - 1, 0 : nx - 1, low])

    def gather_row_high(sems):
        landed(sems[1], row_src.at[0, 0 : nx - 1])
        r = new_recv()
        s = new_send(row_src.at[0 : ny - 1, :, high])
        for d in near_first(ny):
            push(row_src.at[y, :, high], row_src.at[y, :, high], y_at(d)[1], s, r)
        return r

    def gather_row_pass(sems, d):
        y_recv, _, r, s = sems
        src = (y + ny - d) % ny
        landed(y_recv + d, row_src.at[src, x, low])
        for e in far_first(nx):
            push(row_src.at[src, x, low], row_src.at[src, x, low], x_at(e)[1], s, r)

    def gather_row_finish(sems, high_recv):
        landed(sems[2], row_src.at[0 : ny - 1, 0 : nx - 1, low])
        landed(high_recv, row_src.at[0 : ny - 1, :, high])

    unroll = 32

    def spread_forward(rnd):
        src = col_src[rnd]

        def some(turn, acc):
            for i in range(unroll):
                k = turn * unroll + i
                c = meta[1, k]
                d = jnp.dot(tiles[meta[0, k]], src[c // 2, c % 2], preferred_element_type=F32)
                acc = jnp.where(meta[2, k] > 0, d, acc + d)
                part[k] = acc.astype(BF)
            return acc

        lax.fori_loop(0, slots // unroll, some, jnp.zeros((height, height), F32))

        def place(b, _):
            send_f[rnd, b // nx, b % nx] = part[meta[3, b]]
            return 0

        lax.fori_loop(0, nx * ny, place, 0)

    def spread_backward():
        def some(turn, acc):
            for i in range(unroll):
                k = turn * unroll + i
                r = meta[5, k]
                d = jnp.dot(row_src[r // nx, r % nx], tiles[meta[4, k]], preferred_element_type=F32)
                acc = jnp.where(meta[6, k] > 0, d, acc + d)
                part[k] = acc.astype(BF)
            return acc

        lax.fori_loop(0, slots // unroll, some, jnp.zeros((height, height), F32))

        def place(b, _):
            send_b[b // 2, b % 2] = part[meta[7, b]]
            return 0

        lax.fori_loop(0, nz * 2, place, 0)

    y_turns = far_first(ny) + [0]

    def reduce_rows_start(rnd):
        buf = send_f.at[rnd]
        a_recv, b_recv = new_recv(ny), new_recv()
        a_send = new_send(rx_a.at[rnd, :, 0 : nx - 1])
        b_send = new_send(ry_b.at[rnd, 0 : ny - 1])
        for i, dy in enumerate(y_turns):
            for dx in far_first(nx):
                px, peer = x_at(dx)
                push(buf.at[(y + dy) % ny, px, low], rx_a.at[rnd, dy, x], peer, a_send, a_recv + dy)
            if i < ny - 1:
                py, peer = y_at(dy)
                push(buf.at[py, :, high], ry_b.at[rnd, y], peer, b_send, b_recv)
        ya_recv, ya_send = new_recv(), new_send(ry_a.at[rnd, 0 : ny - 1])
        return a_recv, b_recv, ya_recv, ya_send

    def reduce_rows_pass(rnd, sems, dy):
        a_recv, _, ya_recv, ya_send = sems
        landed(a_recv + dy, rx_a.at[rnd, dy, 0 : nx - 1])
        total = send_f[rnd, (y + dy) % ny, x, 0:CUT].astype(F32)
        for dx in near_first(nx):
            total += rx_a[rnd, dy, (x + dx) % nx].astype(F32)
        if dy == 0:
            mid_a[rnd, 0] = total
        else:
            mid = ry_a.at[rnd, ny + dy]
            mid[...] = total.astype(BF)
            push(mid, ry_a.at[rnd, y], y_at(dy)[1], ya_send, ya_recv)

    def reduce_rows_high(rnd, sems):
        landed(sems[1], ry_b.at[rnd, 0 : ny - 1])
        r, s = new_recv(), new_send(rx_b.at[rnd, 0 : nx - 1])
        for dx in far_first(nx) + [0]:
            px = (x + dx) % nx
            total = send_f[rnd, y, px, CUT:height].astype(F32)
            for dy in near_first(ny):
                total += ry_b[rnd, (y + dy) % ny, px].astype(F32)
            if dx == 0:
                mid_b[rnd, 0] = total
            else:
                mid = rx_b.at[rnd, nx + dx]
                mid[...] = total.astype(BF)
                push(mid, rx_b.at[rnd, x], x_at(dx)[1], s, r)
        return r

    def reduce_rows_finish(rnd, sems, high_recv):
        landed(high_recv, rx_b.at[rnd, 0 : nx - 1])
        bottom = mid_b[rnd, 0]
        for dx in near_first(nx):
            bottom += rx_b[rnd, (x + dx) % nx].astype(F32)
        landed(sems[2], ry_a.at[rnd, 0 : ny - 1])
        top = mid_a[rnd, 0]
        for dy in near_first(ny):
            top += ry_a[rnd, (y + dy) % ny].astype(F32)
        return jnp.concatenate([top, bottom], axis=0)

    def reduce_cols_start():
        r = new_recv()
        push(send_b.at[:, 1 - core], r_core, sibling, new_send(r_core), r)
        return r

    def reduce_cols_second(recv):
        landed(recv, r_core)
        r, s = new_recv(), new_send(r_z.at[0 : nz - 1])
        for d in near_first(nz):
            pz, peer = z_at(d)
            mid_z[pz] = (send_b[pz, core].astype(F32) + r_core[pz].astype(F32)).astype(BF)
            push(mid_z.at[pz], r_z.at[z], peer, s, r)
        return r

    def reduce_cols_finish(recv):
        total = send_b[z, core].astype(F32) + r_core[z].astype(F32)
        landed(recv, r_z.at[0 : nz - 1])
        for d in near_first(nz):
            total += r_z[(z + d) % nz].astype(F32)
        return total.astype(BF)

    part[slots] = jnp.zeros((height, height), BF)
    loads["cot"].wait()
    loads["own"].wait()
    row_src[y, x] = cot[...].astype(F32).T.astype(BF)
    pl.semaphore_wait(barrier, len(everyone))

    col_sems = gather_col_start(0)
    row_sems = gather_row_start()
    loads["rows"].wait()
    loads["cols"].wait()
    loads["count"].wait()
    live = count[0, 0]
    meta_v[...] = jnp.zeros_like(meta_v)
    for i, line in enumerate(slot_order(rows[0], cols[0], live, nx * ny) + slot_order(cols[0], rows[0], live, nz * 2)):
        meta_v[i : i + 1, 0:slots] = line
    meta_copy = pltpu.make_async_copy(meta_v, meta, local_sem.at[8])
    meta_copy.start()
    high_recv = gather_row_high(row_sems)
    for i in range(1, max(ny, nz)):
        if i < nz:
            gather_col_pass(0, col_sems, near_first(nz)[i - 1])
        if i < ny:
            gather_row_pass(row_sems, near_first(ny)[i - 1])
    meta_copy.wait()
    loads["tiles"].wait()
    gather_col_finish(0, col_sems)
    spread_forward(0)
    sum_sems = reduce_rows_start(0)
    gather_row_finish(row_sems, high_recv)
    spread_backward()
    core_recv = reduce_cols_start()
    for dy in y_turns[0:2]:
        reduce_rows_pass(0, sum_sems, dy)
    z_recv = reduce_cols_second(core_recv)
    for dy in y_turns[2:]:
        reduce_rows_pass(0, sum_sems, dy)
    high_recv = reduce_rows_high(0, sum_sems)
    loads["w_in"].wait()
    loads["w_hid"].wait()
    mixed = reduce_rows_finish(0, sum_sems, high_recv)
    sum_first = split_dot(mixed, w_in[...])
    col_src_1[z, core] = (sum_first / (1.0 + jnp.exp(-sum_first))).astype(BF)

    col_sems = gather_col_start(1)
    mixed_t = mixed.T.astype(BF)
    sum_t = sum_first.T
    gate_t = 1.0 / (1.0 + jnp.exp(-sum_t))
    hidden_t = (sum_t * gate_t).astype(BF)
    slope_t = gate_t * (1.0 + sum_t * (1.0 - gate_t))
    grad_t = reduce_cols_finish(z_recv)
    grad_sum_t = (jnp.dot(w_hid[...], grad_t, preferred_element_type=F32) * slope_t).astype(BF)
    term[0:height] = lax.dot_general(mixed_t, grad_sum_t, CONTRACT_LAST, preferred_element_type=F32).astype(BF)
    term[height : 2 * height] = lax.dot_general(
        hidden_t, grad_t, CONTRACT_LAST, preferred_element_type=F32
    ).astype(BF)
    band = 2 * height // nx

    def rows_of(i):
        return pl.ds(pl.multiple_of(i * band, band), band)

    r_x, s_x = new_recv(), new_send(ar_x.at[0 : nx - 1])
    for d in far_first(nx):
        push(term.at[rows_of(x_at(d)[0])], ar_x.at[x], x_at(d)[1], s_x, r_x)
    for d in near_first(nz)[0:3]:
        gather_col_pass(1, col_sems, d)
    landed(r_x, ar_x.at[0 : nx - 1])
    total = term[rows_of(x)].astype(F32)
    for d in near_first(nx):
        total += ar_x[(x + d) % nx].astype(F32)
    ar_y[y] = total.astype(BF)
    r_y, s_y = new_recv(), new_send(ar_y.at[0 : ny - 1])
    for d in far_first(ny):
        push(ar_y.at[y], ar_y.at[y], y_at(d)[1], s_y, r_y)
    for d in near_first(nz)[3:]:
        gather_col_pass(1, col_sems, d)
    gather_col_finish(1, col_sems)
    spread_forward(1)
    sum_sems = reduce_rows_start(1)
    landed(r_y, ar_y.at[0 : ny - 1])
    total = ar_y[0].astype(F32)
    for i in range(1, ny):
        total += ar_y[i].astype(F32)
    ar_core[core] = total.astype(BF)
    r_core_sum = new_recv()
    push(ar_core.at[core], ar_core.at[core], sibling, new_send(ar_core.at[0]), r_core_sum)
    for dy in y_turns[0:1]:
        reduce_rows_pass(1, sum_sems, dy)
    landed(r_core_sum, ar_core.at[0])
    ar_z[z] = (ar_core[0].astype(F32) + ar_core[1].astype(F32)).astype(BF)
    r_last, s_last = new_recv(), new_send(ar_z.at[0 : nz - 1])
    for d in far_first(nz):
        push(ar_z.at[z], ar_z.at[z], z_at(d)[1], s_last, r_last)
    for dy in y_turns[1:]:
        reduce_rows_pass(1, sum_sems, dy)
    high_recv = reduce_rows_high(1, sum_sems)
    landed(r_last, ar_z.at[0 : nz - 1])
    total = ar_z[0].astype(F32)
    for i in range(1, nz):
        total += ar_z[i].astype(F32)
    ar_out[rows_of(x)] = total.astype(BF)
    r_out, s_out = new_recv(), new_send(ar_out.at[0 : 2 * height - band])
    for d in far_first(nx):
        push(ar_out.at[rows_of(x)], ar_out.at[rows_of(x)], x_at(d)[1], s_out, r_out)
    logits[...] = split_dot(reduce_rows_finish(1, sum_sems, high_recv), w_hid[...])
    landed(r_out, ar_out.at[0 : 2 * height - band])
    gw_in[...] = ar_out[0:height].astype(F32)
    gw_hid[...] = ar_out[height : 2 * height].astype(F32)

    for s, ref in sends:
        pltpu.make_async_copy(ref, ref, ssem.at[s]).wait()


def write_out(a, b, c, a_out, b_out, c_out, sem):
    copies = [pltpu.make_async_copy(s, d, sem.at[i]) for i, (s, d) in enumerate([(a, a_out), (b, b_out), (c, c_out)])]
    for copy in copies:
        copy.start()
    for copy in copies:
        copy.wait()


def body(nx, features, weight_in, weight_hidden, tile_rows, tile_cols, tile_values, tile_counts, cotangent):
    nz = lax.axis_size("row") // 2
    ny = lax.axis_size(("col", "rep")) // nx
    slots, height = tile_values.shape[2], tile_values.shape[3]
    rest = height - CUT
    band = 2 * height // nx
    block = (height, height)
    vmem = pl.BlockSpec(memory_space=pltpu.VMEM)
    hbm = pl.BlockSpec(memory_space=pltpu.HBM)
    results = [jax.ShapeDtypeStruct(block, F32)] * 3
    outs = pl.pallas_call(
        functools.partial(kernel, nx, ny, nz, slots),
        out_shape=results,
        in_specs=[hbm] * 8,
        out_specs=[vmem] * 3,
        scratch_shapes=[
            pltpu.VMEM(block, BF),
            pltpu.VMEM(block, BF),
            pltpu.VMEM((1, 1, slots), I32),
            pltpu.VMEM((1, 1, slots), I32),
            pltpu.VMEM((slots,) + block, BF),
            pltpu.SMEM((1, 1), I32),
            pltpu.VMEM(block, BF),
            pltpu.VMEM((8, 128), I32),
            pltpu.SMEM((8, 128), I32),
            pltpu.VMEM((nz, 2) + block, BF),
            pltpu.VMEM((nz, 2) + block, BF),
            pltpu.VMEM((ny, nx) + block, BF),
            pltpu.VMEM((slots + 1,) + block, BF),
            pltpu.VMEM((2, ny, nx) + block, BF),
            pltpu.VMEM((2, ny, nx, CUT, height), BF),
            pltpu.VMEM((2, 2 * nx, rest, height), BF),
            pltpu.VMEM((2, 1, CUT, height), F32),
            pltpu.VMEM((2, 1, rest, height), F32),
            pltpu.VMEM((2, 2 * ny, CUT, height), BF),
            pltpu.VMEM((2, ny, nx, rest, height), BF),
            pltpu.VMEM((nz, 2) + block, BF),
            pltpu.VMEM((nz,) + block, BF),
            pltpu.VMEM((nz,) + block, BF),
            pltpu.VMEM((nz,) + block, BF),
            pltpu.VMEM((2 * height, height), BF),
            pltpu.VMEM((nx, band, height), BF),
            pltpu.VMEM((ny, band, height), BF),
            pltpu.VMEM((2, band, height), BF),
            pltpu.VMEM((nz, band, height), BF),
            pltpu.VMEM((2 * height, height), BF),
            pltpu.SemaphoreType.DMA((9,)),
            pltpu.SemaphoreType.DMA((40,)),
            pltpu.SemaphoreType.DMA((72,)),
        ],
        compiler_params=pltpu.CompilerParams(
            collective_id=0, has_side_effects=True, vmem_limit_bytes=56 * 1024 * 1024
        ),
    )(
        features, weight_in, weight_hidden, tile_rows, tile_cols,
        tile_values.reshape((slots,) + block), tile_counts, cotangent,
    )
    return pl.pallas_call(
        write_out,
        out_shape=results,
        in_specs=[vmem] * 3,
        out_specs=[hbm] * 3,
        scratch_shapes=[pltpu.SemaphoreType.DMA((3,))],
    )(*outs)


def solution(mesh, nx=4):
    return jax.shard_map(
        functools.partial(body, nx),
        mesh=mesh,
        in_specs=(
            P(("row", "col", "rep"), None),
            P(),
            P(),
            P("row", ("col", "rep"), None),
            P("row", ("col", "rep"), None),
            P("row", ("col", "rep"), None, None, None),
            P("row", ("col", "rep")),
            P(("row", "col", "rep"), None),
        ),
        out_specs=(P(("row", "col", "rep"), None), P(), P()),
        check_vma=False,
    )
```

```python
import functools

import jax
import jax.numpy as jnp
from jax import lax
from jax.experimental import pallas as pl
from jax.experimental.pallas import tpu as pltpu
from jax.sharding import PartitionSpec as P

MESH = pl.DeviceIdType.MESH
BF = jnp.bfloat16
F32 = jnp.float32
I32 = jnp.int32
CONTRACT_LAST = (((1,), (1,)), ((), ()))
CUT = 96


def near_first(n):
    return sorted(range(1, n), key=lambda d: (min(d, n - d), d))


def far_first(n):
    return near_first(n)[::-1]


def split_dot(wide, weight):
    head = wide.astype(BF)
    rest = (wide - head.astype(F32)).astype(BF)
    return jnp.dot(head, weight, preferred_element_type=F32) + jnp.dot(rest, weight, preferred_element_type=F32)


def slot_order(group, other, count, groups):
    slots = group.shape[1]
    down = lax.broadcasted_iota(I32, (slots, slots), 0)
    along = lax.broadcasted_iota(I32, (slots, slots), 1)
    live = along < count

    def upright(row):
        return jnp.sum(jnp.where(down == along, row, 0), axis=1, keepdims=True)

    key = jnp.where(live, jnp.broadcast_to(group, (slots, slots)), groups)
    key_down = upright(key)
    other_down = upright(jnp.where(live, jnp.broadcast_to(other, (slots, slots)), 0))
    ahead = jnp.where((key == key_down) & (along < down), 1, 0)
    rank = jnp.sum(jnp.where(key < key_down, 1, ahead), axis=1, keepdims=True)
    opens = jnp.where(jnp.sum(ahead, axis=1, keepdims=True) == 0, 1, 0)
    here = rank == along

    def placed(value):
        return jnp.sum(jnp.where(here, value, 0), axis=0, keepdims=True)

    upto = jnp.sum(jnp.where(key_down <= along, 1, 0), axis=0, keepdims=True)
    found = jnp.sum(jnp.where(key_down == along, 1, 0), axis=0, keepdims=True)
    last = jnp.where(found > 0, upto - 1, slots)
    return placed(down), placed(other_down), placed(opens), last


def kernel(
    nx, ny, nz, slots,
    feat_hbm, w_in_hbm, w_hid_hbm, rows_hbm, cols_hbm, tiles_hbm, count_hbm, cot_hbm,
    logits, gw_in, gw_hid,
    w_in, w_hid, rows, cols, tiles, count, cot, meta_v, meta,
    col_src_0, col_src_1, row_src, part, send_f, rx_a, rx_b, mid_a, mid_b, ry_a, ry_b,
    send_b, r_core, mid_z, r_z, term, ar_x, ar_y, ar_core, ar_z, ar_out,
    local_sem, ssem, rsem,
):
    row = lax.axis_index("row")
    col = lax.axis_index("col")
    rep = lax.axis_index("rep")
    reps_y = lax.axis_size("rep") // nx
    z, core = row // 2, row % 2
    y, x = col * reps_y + rep // nx, rep % nx
    height = cot.shape[0]
    rest = height - CUT
    high, low = pl.ds(0, rest), pl.ds(rest, CUT)
    pieces = (((0, CUT // 2), (CUT // 2, CUT // 2)), ((0, CUT),))
    early = rest + CUT // 2
    col_src = (col_src_0, col_src_1)

    def device(xx, yy, zz, cc):
        return (zz * 2 + cc, yy // reps_y, (yy % reps_y) * nx + xx)

    def x_at(d):
        return (x + d) % nx, device((x + d) % nx, y, z, core)

    def y_at(d):
        return (y + d) % ny, device(x, (y + d) % ny, z, core)

    def z_at(d):
        return (z + d) % nz, device(x, y, (z + d) % nz, core)

    sibling = device(x, y, z, 1 - core)

    loads = {}
    for i, (name, src, dst) in enumerate([
        ("cot", cot_hbm, cot), ("own", feat_hbm, col_src_0.at[z, core]), ("rows", rows_hbm, rows),
        ("cols", cols_hbm, cols), ("count", count_hbm, count), ("w_in", w_in_hbm, w_in),
        ("w_hid", w_hid_hbm, w_hid), ("tiles", tiles_hbm, tiles),
    ]):
        loads[name] = pltpu.make_async_copy(src, dst, local_sem.at[i])
        loads[name].start()

    barrier = pltpu.get_barrier_semaphore()
    everyone = [x_at(d)[1] for d in near_first(nx)] + [y_at(d)[1] for d in near_first(ny)]
    everyone += [z_at(d)[1] for d in near_first(nz)] + [sibling]
    for peer in everyone:
        pl.semaphore_signal(barrier, inc=1, device_id=peer, device_id_type=MESH)

    sends = []
    used = [0, 0]

    def new_recv(n=1):
        used[0] += n
        return used[0] - n

    def new_send(ref):
        sends.append((used[1], ref))
        used[1] += 1
        return used[1] - 1

    def push(src, dst, peer, s, r):
        pltpu.make_async_remote_copy(
            src_ref=src, dst_ref=dst, send_sem=ssem.at[s], recv_sem=rsem.at[r],
            device_id=peer, device_id_type=MESH,
        ).start()

    def landed(r, ref):
        pltpu.make_async_copy(ref, ref, rsem.at[r]).wait()

    def gather_col_start(rnd, *cuts):
        buf = col_src[rnd]
        runs = [(pl.ds(*cut), new_recv(nz), new_send(buf.at[0 : nz - 1, 0, pl.ds(*cut)])) for cut in cuts]
        return runs, new_recv(), new_send(buf.at[:, 0])

    def gather_col_run(rnd, sems, i):
        buf = col_src[rnd]
        runs, c_recv, c_send = sems
        some, z_recv, s = runs[i]
        for d in near_first(nz):
            push(buf.at[z, core, some], buf.at[z, core, some], z_at(d)[1], s, z_recv + d)
        push(buf.at[z, core, some], buf.at[z, core, some], sibling, c_send, c_recv)

    def gather_col_pass(rnd, sems, d):
        buf = col_src[rnd]
        runs, c_recv, c_send = sems
        src = (z + nz - d) % nz
        for some, z_recv, _ in runs:
            landed(z_recv + d, buf.at[src, core, some])
        push(buf.at[src, core], buf.at[src, core], sibling, c_send, c_recv)

    def gather_col_finish(rnd, sems):
        landed(sems[1], col_src[rnd].at[:, 0])

    def gather_row_start():
        y_recv = new_recv(ny)
        s = new_send(row_src.at[0 : ny - 1, 0, low])
        for d in near_first(ny):
            push(row_src.at[y, x, low], row_src.at[y, x, low], y_at(d)[1], s, y_recv + d)
        x_recv = new_recv()
        s = new_send(row_src.at[0, 0 : nx - 1])
        for d in near_first(nx):
            push(row_src.at[y, x], row_src.at[y, x], x_at(d)[1], s, x_recv)
        return y_recv, x_recv, new_recv(), new_send(row_src.at[0 : ny - 1, 0 : nx - 1, low])

    def gather_row_high(sems):
        landed(sems[1], row_src.at[0, 0 : nx - 1])
        r = new_recv()
        s = new_send(row_src.at[0 : ny - 1, :, high])
        for d in near_first(ny):
            push(row_src.at[y, :, high], row_src.at[y, :, high], y_at(d)[1], s, r)
        return r

    def gather_row_pass(sems, d):
        y_recv, _, r, s = sems
        src = (y + ny - d) % ny
        landed(y_recv + d, row_src.at[src, x, low])
        for e in far_first(nx):
            push(row_src.at[src, x, low], row_src.at[src, x, low], x_at(e)[1], s, r)

    def gather_row_finish(sems, high_recv):
        landed(sems[2], row_src.at[0 : ny - 1, 0 : nx - 1, low])
        landed(high_recv, row_src.at[0 : ny - 1, :, high])

    unroll = 32

    def spread_forward(rnd):
        src = col_src[rnd]

        def some(turn, acc):
            for i in range(unroll):
                k = turn * unroll + i
                c = meta[1, k]
                d = jnp.dot(tiles[meta[0, k]], src[c // 2, c % 2], preferred_element_type=F32)
                acc = jnp.where(meta[2, k] > 0, d, acc + d)
                part[k] = acc.astype(BF)
            return acc

        lax.fori_loop(0, slots // unroll, some, jnp.zeros((height, height), F32))

        def place(b, _):
            send_f[rnd, b // nx, b % nx] = part[meta[3, b]]
            return 0

        lax.fori_loop(0, nx * ny, place, 0)

    def spread_backward():
        def some(turn, acc):
            for i in range(unroll):
                k = turn * unroll + i
                r = meta[5, k]
                d = jnp.dot(row_src[r // nx, r % nx], tiles[meta[4, k]], preferred_element_type=F32)
                acc = jnp.where(meta[6, k] > 0, d, acc + d)
                part[k] = acc.astype(BF)
            return acc

        lax.fori_loop(0, slots // unroll, some, jnp.zeros((height, height), F32))

        def place(b, _):
            send_b[b // 2, b % 2] = part[meta[7, b]]
            return 0

        lax.fori_loop(0, nz * 2, place, 0)

    y_turns = far_first(ny) + [0]

    def reduce_rows_start(rnd):
        buf = send_f.at[rnd]
        b_recv, b_send = new_recv(), new_send(ry_b.at[rnd, 0 : ny - 1])
        sems = []
        for j, (first, count) in enumerate(pieces[rnd]):
            a_recv, a_send = new_recv(ny), new_send(rx_a.at[rnd, :, 0 : nx - 1, pl.ds(first, count)])
            for i, dy in enumerate(y_turns):
                for dx in far_first(nx):
                    px, peer = x_at(dx)
                    push(
                        buf.at[(y + dy) % ny, px, pl.ds(rest + first, count)],
                        rx_a.at[rnd, dy, x, pl.ds(first, count)], peer, a_send, a_recv + dy,
                    )
                if i < ny - 1 and j == 0:
                    py, peer = y_at(dy)
                    push(buf.at[py, :, high], ry_b.at[rnd, y], peer, b_send, b_recv)
            sems.append((a_recv, new_recv(), new_send(ry_a.at[rnd, 0 : ny - 1, pl.ds(first, count)])))
        return sems, b_recv

    def reduce_rows_pass(rnd, sems, dy, j=0):
        a_recv, ya_recv, ya_send = sems[0][j]
        first, count = pieces[rnd][j]
        some = pl.ds(first, count)
        landed(a_recv + dy, rx_a.at[rnd, dy, 0 : nx - 1, some])
        total = send_f[rnd, (y + dy) % ny, x, pl.ds(rest + first, count)].astype(F32)
        for dx in near_first(nx):
            total += rx_a[rnd, dy, (x + dx) % nx, some].astype(F32)
        if dy == 0:
            mid_a[rnd, 0, some] = total
        else:
            mid = ry_a.at[rnd, ny + dy, some]
            mid[...] = total.astype(BF)
            push(mid, ry_a.at[rnd, y, some], y_at(dy)[1], ya_send, ya_recv)

    def reduce_rows_high(rnd, sems):
        landed(sems[1], ry_b.at[rnd, 0 : ny - 1])
        r, s = new_recv(), new_send(rx_b.at[rnd, 0 : nx - 1])
        for dx in far_first(nx) + [0]:
            px = (x + dx) % nx
            total = send_f[rnd, y, px, 0:rest].astype(F32)
            for dy in near_first(ny):
                total += ry_b[rnd, (y + dy) % ny, px].astype(F32)
            if dx == 0:
                mid_b[rnd, 0] = total
            else:
                mid = rx_b.at[rnd, nx + dx]
                mid[...] = total.astype(BF)
                push(mid, rx_b.at[rnd, x], x_at(dx)[1], s, r)
        return r

    def reduce_rows_finish_high(rnd, high_recv):
        landed(high_recv, rx_b.at[rnd, 0 : nx - 1])
        total = mid_b[rnd, 0]
        for dx in near_first(nx):
            total += rx_b[rnd, (x + dx) % nx].astype(F32)
        return total

    def reduce_rows_finish_low(rnd, sems, j=0):
        first, count = pieces[rnd][j]
        some = pl.ds(first, count)
        landed(sems[0][j][1], ry_a.at[rnd, 0 : ny - 1, some])
        total = mid_a[rnd, 0, some]
        for dy in near_first(ny):
            total += ry_a[rnd, (y + dy) % ny, some].astype(F32)
        return total

    def reduce_cols_start():
        r = new_recv()
        push(send_b.at[:, 1 - core], r_core, sibling, new_send(r_core), r)
        return r

    def reduce_cols_second(recv):
        landed(recv, r_core)
        r, s = new_recv(), new_send(r_z.at[0 : nz - 1])
        for d in near_first(nz):
            pz, peer = z_at(d)
            mid_z[pz] = (send_b[pz, core].astype(F32) + r_core[pz].astype(F32)).astype(BF)
            push(mid_z.at[pz], r_z.at[z], peer, s, r)
        return r

    def reduce_cols_finish(recv):
        total = send_b[z, core].astype(F32) + r_core[z].astype(F32)
        landed(recv, r_z.at[0 : nz - 1])
        for d in near_first(nz):
            total += r_z[(z + d) % nz].astype(F32)
        return total.astype(BF)

    part[slots] = jnp.zeros((height, height), BF)
    loads["cot"].wait()
    loads["own"].wait()
    row_src[y, x] = cot[...].astype(F32).T.astype(BF)
    pl.semaphore_wait(barrier, len(everyone))

    col_sems = gather_col_start(0, (0, height))
    gather_col_run(0, col_sems, 0)
    row_sems = gather_row_start()
    loads["rows"].wait()
    loads["cols"].wait()
    loads["count"].wait()
    live = count[0, 0]
    meta_v[...] = jnp.zeros_like(meta_v)
    for i, line in enumerate(slot_order(rows[0], cols[0], live, nx * ny) + slot_order(cols[0], rows[0], live, nz * 2)):
        meta_v[i : i + 1, 0:slots] = line
    meta_copy = pltpu.make_async_copy(meta_v, meta, local_sem.at[8])
    meta_copy.start()
    high_recv = gather_row_high(row_sems)
    for i in range(1, max(ny, nz)):
        if i < nz:
            gather_col_pass(0, col_sems, near_first(nz)[i - 1])
        if i < ny:
            gather_row_pass(row_sems, near_first(ny)[i - 1])
    meta_copy.wait()
    loads["tiles"].wait()
    gather_col_finish(0, col_sems)
    spread_forward(0)
    sum_sems = reduce_rows_start(0)
    gather_row_finish(row_sems, high_recv)
    spread_backward()
    core_recv = reduce_cols_start()
    for dy in y_turns[0:2]:
        reduce_rows_pass(0, sum_sems, dy)
    z_recv = reduce_cols_second(core_recv)
    for dy in y_turns[2:]:
        reduce_rows_pass(0, sum_sems, dy)
    for dy in y_turns[:2]:
        reduce_rows_pass(0, sum_sems, dy, 1)
    high_recv = reduce_rows_high(0, sum_sems)
    for dy in y_turns[2:7]:
        reduce_rows_pass(0, sum_sems, dy, 1)
    loads["w_in"].wait()
    loads["w_hid"].wait()

    col_sems = gather_col_start(1, (0, early), (early, height - early))

    def activate(mixed):
        sums = split_dot(mixed, w_in[...])
        return sums, (sums / (1.0 + jnp.exp(-sums))).astype(BF)

    mixed_high = reduce_rows_finish_high(0, high_recv)
    mixed_early = jnp.concatenate([mixed_high, reduce_rows_finish_low(0, sum_sems, 0)], axis=0)
    sum_early, hidden_early = activate(mixed_early)
    col_src_1[z, core, 0:early] = hidden_early
    gather_col_run(1, col_sems, 0)
    for dy in y_turns[7:]:
        reduce_rows_pass(0, sum_sems, dy, 1)
    mixed_late = reduce_rows_finish_low(0, sum_sems, 1)
    sum_late, hidden_late = activate(mixed_late)
    col_src_1[z, core, early:height] = hidden_late
    gather_col_run(1, col_sems, 1)
    mixed = jnp.concatenate([mixed_early, mixed_late], axis=0)
    sum_first = jnp.concatenate([sum_early, sum_late], axis=0)

    mixed_t = mixed.T.astype(BF)
    sum_t = sum_first.T
    gate_t = 1.0 / (1.0 + jnp.exp(-sum_t))
    hidden_t = (sum_t * gate_t).astype(BF)
    slope_t = gate_t * (1.0 + sum_t * (1.0 - gate_t))
    grad_t = reduce_cols_finish(z_recv)
    grad_sum_t = (jnp.dot(w_hid[...], grad_t, preferred_element_type=F32) * slope_t).astype(BF)
    term[0:height] = lax.dot_general(mixed_t, grad_sum_t, CONTRACT_LAST, preferred_element_type=F32).astype(BF)
    term[height : 2 * height] = lax.dot_general(
        hidden_t, grad_t, CONTRACT_LAST, preferred_element_type=F32
    ).astype(BF)
    band = 2 * height // nx

    def rows_of(i):
        return pl.ds(pl.multiple_of(i * band, band), band)

    r_x, s_x = new_recv(), new_send(ar_x.at[0 : nx - 1])
    for d in far_first(nx):
        push(term.at[rows_of(x_at(d)[0])], ar_x.at[x], x_at(d)[1], s_x, r_x)
    for d in near_first(nz)[0:3]:
        gather_col_pass(1, col_sems, d)
    landed(r_x, ar_x.at[0 : nx - 1])
    total = term[rows_of(x)].astype(F32)
    for d in near_first(nx):
        total += ar_x[(x + d) % nx].astype(F32)
    ar_y[y] = total.astype(BF)
    r_y, s_y = new_recv(), new_send(ar_y.at[0 : ny - 1])
    for d in far_first(ny):
        push(ar_y.at[y], ar_y.at[y], y_at(d)[1], s_y, r_y)
    for d in near_first(nz)[3:]:
        gather_col_pass(1, col_sems, d)
    gather_col_finish(1, col_sems)
    spread_forward(1)
    sum_sems = reduce_rows_start(1)
    landed(r_y, ar_y.at[0 : ny - 1])
    total = ar_y[0].astype(F32)
    for i in range(1, ny):
        total += ar_y[i].astype(F32)
    ar_core[core] = total.astype(BF)
    r_core_sum = new_recv()
    push(ar_core.at[core], ar_core.at[core], sibling, new_send(ar_core.at[0]), r_core_sum)
    for dy in y_turns[0:1]:
        reduce_rows_pass(1, sum_sems, dy)
    landed(r_core_sum, ar_core.at[0])
    ar_z[z] = (ar_core[0].astype(F32) + ar_core[1].astype(F32)).astype(BF)
    r_last, s_last = new_recv(), new_send(ar_z.at[0 : nz - 1])
    for d in far_first(nz):
        push(ar_z.at[z], ar_z.at[z], z_at(d)[1], s_last, r_last)
    for dy in y_turns[1:-2]:
        reduce_rows_pass(1, sum_sems, dy)
    high_recv = reduce_rows_high(1, sum_sems)
    for dy in y_turns[-2:]:
        reduce_rows_pass(1, sum_sems, dy)
    landed(r_last, ar_z.at[0 : nz - 1])
    total = ar_z[0].astype(F32)
    for i in range(1, nz):
        total += ar_z[i].astype(F32)
    ar_out[rows_of(x)] = total.astype(BF)
    r_out, s_out = new_recv(), new_send(ar_out.at[0 : 2 * height - band])
    for d in far_first(nx):
        push(ar_out.at[rows_of(x)], ar_out.at[rows_of(x)], x_at(d)[1], s_out, r_out)
    mixed = jnp.concatenate([reduce_rows_finish_high(1, high_recv), reduce_rows_finish_low(1, sum_sems)], axis=0)
    logits[...] = split_dot(mixed, w_hid[...])
    landed(r_out, ar_out.at[0 : 2 * height - band])
    gw_in[...] = ar_out[0:height].astype(F32)
    gw_hid[...] = ar_out[height : 2 * height].astype(F32)

    for s, ref in sends:
        pltpu.make_async_copy(ref, ref, ssem.at[s]).wait()


def write_out(a, b, c, a_out, b_out, c_out, sem):
    copies = [pltpu.make_async_copy(s, d, sem.at[i]) for i, (s, d) in enumerate([(a, a_out), (b, b_out), (c, c_out)])]
    for copy in copies:
        copy.start()
    for copy in copies:
        copy.wait()


def body(nx, features, weight_in, weight_hidden, tile_rows, tile_cols, tile_values, tile_counts, cotangent):
    nz = lax.axis_size("row") // 2
    ny = lax.axis_size(("col", "rep")) // nx
    slots, height = tile_values.shape[2], tile_values.shape[3]
    rest = height - CUT
    band = 2 * height // nx
    block = (height, height)
    vmem = pl.BlockSpec(memory_space=pltpu.VMEM)
    hbm = pl.BlockSpec(memory_space=pltpu.HBM)
    results = [jax.ShapeDtypeStruct(block, F32)] * 3
    outs = pl.pallas_call(
        functools.partial(kernel, nx, ny, nz, slots),
        out_shape=results,
        in_specs=[hbm] * 8,
        out_specs=[vmem] * 3,
        scratch_shapes=[
            pltpu.VMEM(block, BF),
            pltpu.VMEM(block, BF),
            pltpu.VMEM((1, 1, slots), I32),
            pltpu.VMEM((1, 1, slots), I32),
            pltpu.VMEM((slots,) + block, BF),
            pltpu.SMEM((1, 1), I32),
            pltpu.VMEM(block, BF),
            pltpu.VMEM((8, 128), I32),
            pltpu.SMEM((8, 128), I32),
            pltpu.VMEM((nz, 2) + block, BF),
            pltpu.VMEM((nz, 2) + block, BF),
            pltpu.VMEM((ny, nx) + block, BF),
            pltpu.VMEM((slots + 1,) + block, BF),
            pltpu.VMEM((2, ny, nx) + block, BF),
            pltpu.VMEM((2, ny, nx, CUT, height), BF),
            pltpu.VMEM((2, 2 * nx, rest, height), BF),
            pltpu.VMEM((2, 1, CUT, height), F32),
            pltpu.VMEM((2, 1, rest, height), F32),
            pltpu.VMEM((2, 2 * ny, CUT, height), BF),
            pltpu.VMEM((2, ny, nx, rest, height), BF),
            pltpu.VMEM((nz, 2) + block, BF),
            pltpu.VMEM((nz,) + block, BF),
            pltpu.VMEM((nz,) + block, BF),
            pltpu.VMEM((nz,) + block, BF),
            pltpu.VMEM((2 * height, height), BF),
            pltpu.VMEM((nx, band, height), BF),
            pltpu.VMEM((ny, band, height), BF),
            pltpu.VMEM((2, band, height), BF),
            pltpu.VMEM((nz, band, height), BF),
            pltpu.VMEM((2 * height, height), BF),
            pltpu.SemaphoreType.DMA((9,)),
            pltpu.SemaphoreType.DMA((48,)),
            pltpu.SemaphoreType.DMA((88,)),
        ],
        compiler_params=pltpu.CompilerParams(
            collective_id=0, has_side_effects=True, vmem_limit_bytes=56 * 1024 * 1024
        ),
    )(
        features, weight_in, weight_hidden, tile_rows, tile_cols,
        tile_values.reshape((slots,) + block), tile_counts, cotangent,
    )
    return pl.pallas_call(
        write_out,
        out_shape=results,
        in_specs=[vmem] * 3,
        out_specs=[hbm] * 3,
        scratch_shapes=[pltpu.SemaphoreType.DMA((3,))],
    )(*outs)


def solution(mesh, nx=4):
    return jax.shard_map(
        functools.partial(body, nx),
        mesh=mesh,
        in_specs=(
            P(("row", "col", "rep"), None),
            P(),
            P(),
            P("row", ("col", "rep"), None),
            P("row", ("col", "rep"), None),
            P("row", ("col", "rep"), None, None, None),
            P("row", ("col", "rep")),
            P(("row", "col", "rep"), None),
        ),
        out_specs=(P(("row", "col", "rep"), None), P(), P()),
        check_vma=False,
    )
```

```python
import functools

import jax
import jax.numpy as jnp
from jax import lax
from jax.experimental import pallas as pl
from jax.experimental.pallas import tpu as pltpu
from jax.sharding import PartitionSpec as P

MESH = pl.DeviceIdType.MESH
BF = jnp.bfloat16
F32 = jnp.float32
I32 = jnp.int32
CONTRACT_LAST = (((1,), (1,)), ((), ()))
CUT = 96


def near_first(n):
    return sorted(range(1, n), key=lambda d: (min(d, n - d), d))


def far_first(n):
    return near_first(n)[::-1]


def split_dot(wide, weight):
    head = wide.astype(BF)
    rest = (wide - head.astype(F32)).astype(BF)
    return jnp.dot(head, weight, preferred_element_type=F32) + jnp.dot(rest, weight, preferred_element_type=F32)


def slot_order(group, other, count, groups):
    slots = group.shape[1]
    down = lax.broadcasted_iota(I32, (slots, slots), 0)
    along = lax.broadcasted_iota(I32, (slots, slots), 1)
    live = along < count

    def upright(row):
        return jnp.sum(jnp.where(down == along, row, 0), axis=1, keepdims=True)

    key = jnp.where(live, jnp.broadcast_to(group, (slots, slots)), groups)
    key_down = upright(key)
    other_down = upright(jnp.where(live, jnp.broadcast_to(other, (slots, slots)), 0))
    ahead = jnp.where((key == key_down) & (along < down), 1, 0)
    rank = jnp.sum(jnp.where(key < key_down, 1, ahead), axis=1, keepdims=True)
    follows = jnp.where(jnp.sum(ahead, axis=1, keepdims=True) == 0, 0, 1)
    here = rank == along

    def placed(value):
        return jnp.sum(jnp.where(here, value, 0), axis=0, keepdims=True)

    upto = jnp.sum(jnp.where(key_down <= along, 1, 0), axis=0, keepdims=True)
    found = jnp.sum(jnp.where(key_down == along, 1, 0), axis=0, keepdims=True)
    last = jnp.where(found > 0, upto - 1, slots)
    return placed(down), placed(other_down), placed(follows), last


def kernel(
    nx, ny, nz, slots,
    feat_hbm, w_in_hbm, w_hid_hbm, rows_hbm, cols_hbm, tiles_hbm, count_hbm, cot_hbm,
    logits, gw_in, gw_hid,
    w_in, w_hid, rows, cols, tiles, count, cot, meta_v, meta,
    col_src_0, col_src_1, row_src, part, send_f, rx_a, rx_b, mid_a, mid_b, ry_a, ry_b,
    send_b, r_core, mid_z, r_z, term, ar_x, ar_y, ar_core, ar_z, ar_out,
    local_sem, ssem, rsem,
):
    row = lax.axis_index("row")
    col = lax.axis_index("col")
    rep = lax.axis_index("rep")
    reps_y = lax.axis_size("rep") // nx
    z, core = row // 2, row % 2
    y, x = col * reps_y + rep // nx, rep % nx
    height = cot.shape[0]
    rest = height - CUT
    high, low = pl.ds(0, rest), pl.ds(rest, CUT)
    pieces = (((0, CUT // 2), (CUT // 2, CUT // 2)), ((0, CUT),))
    early = rest + CUT // 2
    col_src = (col_src_0, col_src_1)

    def device(xx, yy, zz, cc):
        return (zz * 2 + cc, yy // reps_y, (yy % reps_y) * nx + xx)

    def x_at(d):
        return (x + d) % nx, device((x + d) % nx, y, z, core)

    def y_at(d):
        return (y + d) % ny, device(x, (y + d) % ny, z, core)

    def z_at(d):
        return (z + d) % nz, device(x, y, (z + d) % nz, core)

    sibling = device(x, y, z, 1 - core)

    loads = {}
    for i, (name, src, dst) in enumerate([
        ("cot", cot_hbm, cot), ("own", feat_hbm, col_src_0.at[z, core]), ("rows", rows_hbm, rows),
        ("cols", cols_hbm, cols), ("count", count_hbm, count), ("w_in", w_in_hbm, w_in),
        ("w_hid", w_hid_hbm, w_hid), ("tiles", tiles_hbm, tiles),
    ]):
        loads[name] = pltpu.make_async_copy(src, dst, local_sem.at[i])
        loads[name].start()

    barrier = pltpu.get_barrier_semaphore()
    everyone = [x_at(d)[1] for d in near_first(nx)] + [y_at(d)[1] for d in near_first(ny)]
    everyone += [z_at(d)[1] for d in near_first(nz)] + [sibling]
    for peer in everyone:
        pl.semaphore_signal(barrier, inc=1, device_id=peer, device_id_type=MESH)

    sends = []
    used = [0, 0]

    def new_recv(n=1):
        used[0] += n
        return used[0] - n

    def new_send(ref):
        sends.append((used[1], ref))
        used[1] += 1
        return used[1] - 1

    def push(src, dst, peer, s, r):
        pltpu.make_async_remote_copy(
            src_ref=src, dst_ref=dst, send_sem=ssem.at[s], recv_sem=rsem.at[r],
            device_id=peer, device_id_type=MESH,
        ).start()

    def landed(r, ref):
        pltpu.make_async_copy(ref, ref, rsem.at[r]).wait()

    def gather_col_start(rnd, *cuts):
        buf = col_src[rnd]
        runs = [(pl.ds(*cut), new_recv(nz), new_send(buf.at[0 : nz - 1, 0, pl.ds(*cut)])) for cut in cuts]
        return runs, new_recv(), new_send(buf.at[:, 0])

    def gather_col_run(rnd, sems, i):
        buf = col_src[rnd]
        runs, c_recv, c_send = sems
        some, z_recv, s = runs[i]
        for d in near_first(nz):
            push(buf.at[z, core, some], buf.at[z, core, some], z_at(d)[1], s, z_recv + d)
        push(buf.at[z, core, some], buf.at[z, core, some], sibling, c_send, c_recv)

    def gather_col_pass(rnd, sems, d):
        buf = col_src[rnd]
        runs, c_recv, c_send = sems
        src = (z + nz - d) % nz
        for some, z_recv, _ in runs:
            landed(z_recv + d, buf.at[src, core, some])
        push(buf.at[src, core], buf.at[src, core], sibling, c_send, c_recv)

    def gather_col_finish(rnd, sems):
        landed(sems[1], col_src[rnd].at[:, 0])

    def gather_row_start():
        y_recv = new_recv(ny)
        s = new_send(row_src.at[0 : ny - 1, 0, low])
        for d in near_first(ny):
            push(row_src.at[y, x, low], row_src.at[y, x, low], y_at(d)[1], s, y_recv + d)
        x_recv = new_recv()
        s = new_send(row_src.at[0, 0 : nx - 1])
        for d in near_first(nx):
            push(row_src.at[y, x], row_src.at[y, x], x_at(d)[1], s, x_recv)
        return y_recv, x_recv, new_recv(), new_send(row_src.at[0 : ny - 1, 0 : nx - 1, low])

    def gather_row_high(sems):
        landed(sems[1], row_src.at[0, 0 : nx - 1])
        r = new_recv()
        s = new_send(row_src.at[0 : ny - 1, :, high])
        for d in near_first(ny):
            push(row_src.at[y, :, high], row_src.at[y, :, high], y_at(d)[1], s, r)
        return r

    def gather_row_pass(sems, d):
        y_recv, _, r, s = sems
        src = (y + ny - d) % ny
        landed(y_recv + d, row_src.at[src, x, low])
        for e in far_first(nx):
            push(row_src.at[src, x, low], row_src.at[src, x, low], x_at(e)[1], s, r)

    def gather_row_finish(sems, high_recv):
        landed(sems[2], row_src.at[0 : ny - 1, 0 : nx - 1, low])
        landed(high_recv, row_src.at[0 : ny - 1, :, high])

    unroll = 32

    def spread_forward(rnd):
        src = col_src[rnd]

        def some(turn, acc):
            for i in range(unroll):
                k = turn * unroll + i
                c = meta[1, k]
                d = jnp.dot(tiles[meta[0, k]], src[c // 2, c % 2], preferred_element_type=F32)
                acc = acc * meta[2, k].astype(F32) + d
                part[k] = acc.astype(BF)
            return acc

        lax.fori_loop(0, slots // unroll, some, jnp.zeros((height, height), F32))

        def place(b, _):
            send_f[rnd, b // nx, b % nx] = part[meta[3, b]]
            return 0

        lax.fori_loop(0, nx * ny, place, 0, unroll=8)

    def spread_backward():
        def some(turn, acc):
            for i in range(unroll):
                k = turn * unroll + i
                r = meta[5, k]
                d = jnp.dot(row_src[r // nx, r % nx], tiles[meta[4, k]], preferred_element_type=F32)
                acc = acc * meta[6, k].astype(F32) + d
                part[k] = acc.astype(BF)
            return acc

        lax.fori_loop(0, slots // unroll, some, jnp.zeros((height, height), F32))

        def place(b, _):
            send_b[b // 2, b % 2] = part[meta[7, b]]
            return 0

        lax.fori_loop(0, nz * 2, place, 0, unroll=8)

    y_turns = far_first(ny) + [0]

    def reduce_rows_start(rnd):
        buf = send_f.at[rnd]
        b_recv, b_send = new_recv(), new_send(ry_b.at[rnd, 0 : ny - 1])
        sems = []
        for j, (first, count) in enumerate(pieces[rnd]):
            a_recv, a_send = new_recv(ny), new_send(rx_a.at[rnd, :, 0 : nx - 1, pl.ds(first, count)])
            for i, dy in enumerate(y_turns):
                for dx in far_first(nx):
                    px, peer = x_at(dx)
                    push(
                        buf.at[(y + dy) % ny, px, pl.ds(rest + first, count)],
                        rx_a.at[rnd, dy, x, pl.ds(first, count)], peer, a_send, a_recv + dy,
                    )
                if i < ny - 1 and j == 0:
                    py, peer = y_at(dy)
                    push(buf.at[py, :, high], ry_b.at[rnd, y], peer, b_send, b_recv)
            sems.append((a_recv, new_recv(), new_send(ry_a.at[rnd, 0 : ny - 1, pl.ds(first, count)])))
        return sems, b_recv

    def reduce_rows_pass(rnd, sems, dy, j=0):
        a_recv, ya_recv, ya_send = sems[0][j]
        first, count = pieces[rnd][j]
        some = pl.ds(first, count)
        landed(a_recv + dy, rx_a.at[rnd, dy, 0 : nx - 1, some])
        total = send_f[rnd, (y + dy) % ny, x, pl.ds(rest + first, count)].astype(F32)
        for dx in near_first(nx):
            total += rx_a[rnd, dy, (x + dx) % nx, some].astype(F32)
        if dy == 0:
            mid_a[rnd, 0, some] = total
        else:
            mid = ry_a.at[rnd, ny + dy, some]
            mid[...] = total.astype(BF)
            push(mid, ry_a.at[rnd, y, some], y_at(dy)[1], ya_send, ya_recv)

    def reduce_rows_high(rnd, sems):
        landed(sems[1], ry_b.at[rnd, 0 : ny - 1])
        r, s = new_recv(), new_send(rx_b.at[rnd, 0 : nx - 1])
        for dx in far_first(nx) + [0]:
            px = (x + dx) % nx
            total = send_f[rnd, y, px, 0:rest].astype(F32)
            for dy in near_first(ny):
                total += ry_b[rnd, (y + dy) % ny, px].astype(F32)
            if dx == 0:
                mid_b[rnd, 0] = total
            else:
                mid = rx_b.at[rnd, nx + dx]
                mid[...] = total.astype(BF)
                push(mid, rx_b.at[rnd, x], x_at(dx)[1], s, r)
        return r

    def reduce_rows_finish_high(rnd, high_recv):
        landed(high_recv, rx_b.at[rnd, 0 : nx - 1])
        total = mid_b[rnd, 0]
        for dx in near_first(nx):
            total += rx_b[rnd, (x + dx) % nx].astype(F32)
        return total

    def reduce_rows_finish_low(rnd, sems, j=0):
        first, count = pieces[rnd][j]
        some = pl.ds(first, count)
        landed(sems[0][j][1], ry_a.at[rnd, 0 : ny - 1, some])
        total = mid_a[rnd, 0, some]
        for dy in near_first(ny):
            total += ry_a[rnd, (y + dy) % ny, some].astype(F32)
        return total

    def reduce_cols_start():
        r = new_recv()
        push(send_b.at[:, 1 - core], r_core, sibling, new_send(r_core), r)
        return r

    def reduce_cols_second(recv):
        landed(recv, r_core)
        r, s = new_recv(), new_send(r_z.at[0 : nz - 1])
        for d in near_first(nz):
            pz, peer = z_at(d)
            mid_z[pz] = (send_b[pz, core].astype(F32) + r_core[pz].astype(F32)).astype(BF)
            push(mid_z.at[pz], r_z.at[z], peer, s, r)
        return r

    def reduce_cols_finish(recv):
        total = send_b[z, core].astype(F32) + r_core[z].astype(F32)
        landed(recv, r_z.at[0 : nz - 1])
        for d in near_first(nz):
            total += r_z[(z + d) % nz].astype(F32)
        return total.astype(BF)

    part[slots] = jnp.zeros((height, height), BF)
    loads["cot"].wait()
    loads["own"].wait()
    row_src[y, x] = cot[...].astype(F32).T.astype(BF)
    pl.semaphore_wait(barrier, len(everyone))

    col_sems = gather_col_start(0, (0, height))
    gather_col_run(0, col_sems, 0)
    row_sems = gather_row_start()
    loads["rows"].wait()
    loads["cols"].wait()
    loads["count"].wait()
    live = count[0, 0]
    meta_v[...] = jnp.zeros_like(meta_v)
    for i, line in enumerate(slot_order(rows[0], cols[0], live, nx * ny) + slot_order(cols[0], rows[0], live, nz * 2)):
        meta_v[i : i + 1, 0:slots] = line
    meta_copy = pltpu.make_async_copy(meta_v, meta, local_sem.at[8])
    meta_copy.start()
    high_recv = gather_row_high(row_sems)
    for i in range(1, max(ny, nz)):
        if i < nz:
            gather_col_pass(0, col_sems, near_first(nz)[i - 1])
        if i < ny:
            gather_row_pass(row_sems, near_first(ny)[i - 1])
    meta_copy.wait()
    loads["tiles"].wait()
    gather_col_finish(0, col_sems)
    spread_forward(0)
    sum_sems = reduce_rows_start(0)
    gather_row_finish(row_sems, high_recv)
    spread_backward()
    core_recv = reduce_cols_start()
    for dy in y_turns[0:2]:
        reduce_rows_pass(0, sum_sems, dy)
    z_recv = reduce_cols_second(core_recv)
    for dy in y_turns[2:]:
        reduce_rows_pass(0, sum_sems, dy)
    for dy in y_turns[:2]:
        reduce_rows_pass(0, sum_sems, dy, 1)
    high_recv = reduce_rows_high(0, sum_sems)
    for dy in y_turns[2:7]:
        reduce_rows_pass(0, sum_sems, dy, 1)
    loads["w_in"].wait()
    loads["w_hid"].wait()

    col_sems = gather_col_start(1, (0, early), (early, height - early))

    def activate(mixed):
        sums = split_dot(mixed, w_in[...])
        return sums, (sums / (1.0 + jnp.exp(-sums))).astype(BF)

    mixed_high = reduce_rows_finish_high(0, high_recv)
    mixed_early = jnp.concatenate([mixed_high, reduce_rows_finish_low(0, sum_sems, 0)], axis=0)
    sum_early, hidden_early = activate(mixed_early)
    col_src_1[z, core, 0:early] = hidden_early
    gather_col_run(1, col_sems, 0)
    for dy in y_turns[7:]:
        reduce_rows_pass(0, sum_sems, dy, 1)
    mixed_late = reduce_rows_finish_low(0, sum_sems, 1)
    sum_late, hidden_late = activate(mixed_late)
    col_src_1[z, core, early:height] = hidden_late
    gather_col_run(1, col_sems, 1)
    mixed = jnp.concatenate([mixed_early, mixed_late], axis=0)
    sum_first = jnp.concatenate([sum_early, sum_late], axis=0)

    mixed_t = mixed.T.astype(BF)
    sum_t = sum_first.T
    gate_t = 1.0 / (1.0 + jnp.exp(-sum_t))
    hidden_t = (sum_t * gate_t).astype(BF)
    slope_t = gate_t * (1.0 + sum_t * (1.0 - gate_t))
    grad_t = reduce_cols_finish(z_recv)
    grad_sum_t = (jnp.dot(w_hid[...], grad_t, preferred_element_type=F32) * slope_t).astype(BF)
    term[0:height] = lax.dot_general(mixed_t, grad_sum_t, CONTRACT_LAST, preferred_element_type=F32).astype(BF)
    term[height : 2 * height] = lax.dot_general(
        hidden_t, grad_t, CONTRACT_LAST, preferred_element_type=F32
    ).astype(BF)
    band = 2 * height // nx

    def rows_of(i):
        return pl.ds(pl.multiple_of(i * band, band), band)

    r_x, s_x = new_recv(), new_send(ar_x.at[0 : nx - 1])
    for d in far_first(nx):
        push(term.at[rows_of(x_at(d)[0])], ar_x.at[x], x_at(d)[1], s_x, r_x)
    for d in near_first(nz)[0:3]:
        gather_col_pass(1, col_sems, d)
    landed(r_x, ar_x.at[0 : nx - 1])
    total = term[rows_of(x)].astype(F32)
    for d in near_first(nx):
        total += ar_x[(x + d) % nx].astype(F32)
    ar_y[y] = total.astype(BF)
    r_y, s_y = new_recv(), new_send(ar_y.at[0 : ny - 1])
    for d in far_first(ny):
        push(ar_y.at[y], ar_y.at[y], y_at(d)[1], s_y, r_y)
    for d in near_first(nz)[3:]:
        gather_col_pass(1, col_sems, d)
    gather_col_finish(1, col_sems)
    spread_forward(1)
    sum_sems = reduce_rows_start(1)
    landed(r_y, ar_y.at[0 : ny - 1])
    total = ar_y[0].astype(F32)
    for i in range(1, ny):
        total += ar_y[i].astype(F32)
    ar_core[core] = total.astype(BF)
    r_core_sum = new_recv()
    push(ar_core.at[core], ar_core.at[core], sibling, new_send(ar_core.at[0]), r_core_sum)
    for dy in y_turns[0:1]:
        reduce_rows_pass(1, sum_sems, dy)
    landed(r_core_sum, ar_core.at[0])
    ar_z[z] = (ar_core[0].astype(F32) + ar_core[1].astype(F32)).astype(BF)
    r_last, s_last = new_recv(), new_send(ar_z.at[0 : nz - 1])
    for d in far_first(nz):
        push(ar_z.at[z], ar_z.at[z], z_at(d)[1], s_last, r_last)
    for dy in y_turns[1:-2]:
        reduce_rows_pass(1, sum_sems, dy)
    high_recv = reduce_rows_high(1, sum_sems)
    for dy in y_turns[-2:]:
        reduce_rows_pass(1, sum_sems, dy)
    landed(r_last, ar_z.at[0 : nz - 1])
    total = ar_z[0].astype(F32)
    for i in range(1, nz):
        total += ar_z[i].astype(F32)
    ar_out[rows_of(x)] = total.astype(BF)
    r_out, s_out = new_recv(), new_send(ar_out.at[0 : 2 * height - band])
    for d in far_first(nx):
        push(ar_out.at[rows_of(x)], ar_out.at[rows_of(x)], x_at(d)[1], s_out, r_out)
    mixed = jnp.concatenate([reduce_rows_finish_high(1, high_recv), reduce_rows_finish_low(1, sum_sems)], axis=0)
    logits[...] = split_dot(mixed, w_hid[...])
    landed(r_out, ar_out.at[0 : 2 * height - band])
    gw_in[...] = ar_out[0:height].astype(F32)
    gw_hid[...] = ar_out[height : 2 * height].astype(F32)

    for s, ref in sends:
        pltpu.make_async_copy(ref, ref, ssem.at[s]).wait()


def write_out(a, b, c, a_out, b_out, c_out, sem):
    copies = [pltpu.make_async_copy(s, d, sem.at[i]) for i, (s, d) in enumerate([(a, a_out), (b, b_out), (c, c_out)])]
    for copy in copies:
        copy.start()
    for copy in copies:
        copy.wait()


def body(nx, features, weight_in, weight_hidden, tile_rows, tile_cols, tile_values, tile_counts, cotangent):
    nz = lax.axis_size("row") // 2
    ny = lax.axis_size(("col", "rep")) // nx
    slots, height = tile_values.shape[2], tile_values.shape[3]
    rest = height - CUT
    band = 2 * height // nx
    block = (height, height)
    vmem = pl.BlockSpec(memory_space=pltpu.VMEM)
    hbm = pl.BlockSpec(memory_space=pltpu.HBM)
    results = [jax.ShapeDtypeStruct(block, F32)] * 3
    outs = pl.pallas_call(
        functools.partial(kernel, nx, ny, nz, slots),
        out_shape=results,
        in_specs=[hbm] * 8,
        out_specs=[vmem] * 3,
        scratch_shapes=[
            pltpu.VMEM(block, BF),
            pltpu.VMEM(block, BF),
            pltpu.VMEM((1, 1, slots), I32),
            pltpu.VMEM((1, 1, slots), I32),
            pltpu.VMEM((slots,) + block, BF),
            pltpu.SMEM((1, 1), I32),
            pltpu.VMEM(block, BF),
            pltpu.VMEM((8, 128), I32),
            pltpu.SMEM((8, 128), I32),
            pltpu.VMEM((nz, 2) + block, BF),
            pltpu.VMEM((nz, 2) + block, BF),
            pltpu.VMEM((ny, nx) + block, BF),
            pltpu.VMEM((slots + 1,) + block, BF),
            pltpu.VMEM((2, ny, nx) + block, BF),
            pltpu.VMEM((2, ny, nx, CUT, height), BF),
            pltpu.VMEM((2, 2 * nx, rest, height), BF),
            pltpu.VMEM((2, 1, CUT, height), F32),
            pltpu.VMEM((2, 1, rest, height), F32),
            pltpu.VMEM((2, 2 * ny, CUT, height), BF),
            pltpu.VMEM((2, ny, nx, rest, height), BF),
            pltpu.VMEM((nz, 2) + block, BF),
            pltpu.VMEM((nz,) + block, BF),
            pltpu.VMEM((nz,) + block, BF),
            pltpu.VMEM((nz,) + block, BF),
            pltpu.VMEM((2 * height, height), BF),
            pltpu.VMEM((nx, band, height), BF),
            pltpu.VMEM((ny, band, height), BF),
            pltpu.VMEM((2, band, height), BF),
            pltpu.VMEM((nz, band, height), BF),
            pltpu.VMEM((2 * height, height), BF),
            pltpu.SemaphoreType.DMA((9,)),
            pltpu.SemaphoreType.DMA((48,)),
            pltpu.SemaphoreType.DMA((88,)),
        ],
        compiler_params=pltpu.CompilerParams(
            collective_id=0, has_side_effects=True, vmem_limit_bytes=56 * 1024 * 1024
        ),
    )(
        features, weight_in, weight_hidden, tile_rows, tile_cols,
        tile_values.reshape((slots,) + block), tile_counts, cotangent,
    )
    return pl.pallas_call(
        write_out,
        out_shape=results,
        in_specs=[vmem] * 3,
        out_specs=[hbm] * 3,
        scratch_shapes=[pltpu.SemaphoreType.DMA((3,))],
    )(*outs)


def solution(mesh, nx=4):
    return jax.shard_map(
        functools.partial(body, nx),
        mesh=mesh,
        in_specs=(
            P(("row", "col", "rep"), None),
            P(),
            P(),
            P("row", ("col", "rep"), None),
            P("row", ("col", "rep"), None),
            P("row", ("col", "rep"), None, None, None),
            P("row", ("col", "rep")),
            P(("row", "col", "rep"), None),
        ),
        out_specs=(P(("row", "col", "rep"), None), P(), P()),
        check_vma=False,
    )
```

```python
import functools

import jax
import jax.numpy as jnp
from jax import lax
from jax.experimental import pallas as pl
from jax.experimental.pallas import tpu as pltpu
from jax.sharding import PartitionSpec as P

MESH = pl.DeviceIdType.MESH
BF = jnp.bfloat16
F32 = jnp.float32
I32 = jnp.int32
CONTRACT_LAST = (((1,), (1,)), ((), ()))
CUT = 96


def near_first(n):
    return sorted(range(1, n), key=lambda d: (min(d, n - d), d))


def far_first(n):
    return near_first(n)[::-1]


def split_dot(wide, weight):
    head = wide.astype(BF)
    rest = (wide - head.astype(F32)).astype(BF)
    return jnp.dot(head, weight, preferred_element_type=F32) + jnp.dot(rest, weight, preferred_element_type=F32)


def slot_order(group, other, count, groups):
    slots = group.shape[1]
    down = lax.broadcasted_iota(I32, (slots, slots), 0)
    along = lax.broadcasted_iota(I32, (slots, slots), 1)
    live = along < count

    def upright(row):
        return jnp.sum(jnp.where(down == along, row, 0), axis=1, keepdims=True)

    key = jnp.where(live, jnp.broadcast_to(group, (slots, slots)), groups)
    key_down = upright(key)
    other_down = upright(jnp.where(live, jnp.broadcast_to(other, (slots, slots)), 0))
    ahead = jnp.where((key == key_down) & (along < down), 1, 0)
    rank = jnp.sum(jnp.where(key < key_down, 1, ahead), axis=1, keepdims=True)
    follows = jnp.where(jnp.sum(ahead, axis=1, keepdims=True) == 0, 0, 1)
    here = rank == along

    def placed(value):
        return jnp.sum(jnp.where(here, value, 0), axis=0, keepdims=True)

    upto = jnp.sum(jnp.where(key_down <= along, 1, 0), axis=0, keepdims=True)
    found = jnp.sum(jnp.where(key_down == along, 1, 0), axis=0, keepdims=True)
    last = jnp.where(found > 0, upto - 1, slots)
    return placed(down), placed(other_down), placed(follows), last


def kernel(
    nx, ny, nz, slots,
    feat_hbm, w_in_hbm, w_hid_hbm, rows_hbm, cols_hbm, tiles_hbm, count_hbm, cot_hbm,
    logits, gw_in, gw_hid,
    w_in, w_hid, rows, cols, tiles, count, cot, meta_v, meta,
    col_src_0, col_src_1, row_src, part, send_f, rx_a, rx_b, mid_a, mid_b, ry_a, ry_b,
    send_b, r_core, mid_z, r_z, term, ar_x, ar_y, ar_core, ar_z, ar_out,
    local_sem, ssem, rsem,
):
    row = lax.axis_index("row")
    col = lax.axis_index("col")
    rep = lax.axis_index("rep")
    reps_y = lax.axis_size("rep") // nx
    z, core = row // 2, row % 2
    y, x = col * reps_y + rep // nx, rep % nx
    height = cot.shape[0]
    rest = height - CUT
    high, low = pl.ds(0, rest), pl.ds(rest, CUT)
    pieces = (((0, CUT // 2), (CUT // 2, CUT // 2)), ((0, CUT),))
    early = rest + CUT // 2
    col_src = (col_src_0, col_src_1)

    def device(xx, yy, zz, cc):
        return (zz * 2 + cc, yy // reps_y, (yy % reps_y) * nx + xx)

    def x_at(d):
        return (x + d) % nx, device((x + d) % nx, y, z, core)

    def y_at(d):
        return (y + d) % ny, device(x, (y + d) % ny, z, core)

    def z_at(d):
        return (z + d) % nz, device(x, y, (z + d) % nz, core)

    sibling = device(x, y, z, 1 - core)

    loads = {}
    for i, (name, src, dst) in enumerate([
        ("cot", cot_hbm, cot), ("own", feat_hbm, col_src_0.at[z, core]), ("rows", rows_hbm, rows),
        ("cols", cols_hbm, cols), ("count", count_hbm, count), ("w_in", w_in_hbm, w_in),
        ("w_hid", w_hid_hbm, w_hid), ("tiles", tiles_hbm, tiles),
    ]):
        loads[name] = pltpu.make_async_copy(src, dst, local_sem.at[i])
        loads[name].start()

    barrier = pltpu.get_barrier_semaphore()
    everyone = [x_at(d)[1] for d in near_first(nx)] + [y_at(d)[1] for d in near_first(ny)]
    everyone += [z_at(d)[1] for d in near_first(nz)] + [sibling]
    for peer in everyone:
        pl.semaphore_signal(barrier, inc=1, device_id=peer, device_id_type=MESH)

    sends = []
    used = [0, 0]

    def new_recv(n=1):
        used[0] += n
        return used[0] - n

    def new_send(ref):
        sends.append((used[1], ref))
        used[1] += 1
        return used[1] - 1

    def push(src, dst, peer, s, r):
        pltpu.make_async_remote_copy(
            src_ref=src, dst_ref=dst, send_sem=ssem.at[s], recv_sem=rsem.at[r],
            device_id=peer, device_id_type=MESH,
        ).start()

    def landed(r, ref):
        pltpu.make_async_copy(ref, ref, rsem.at[r]).wait()

    drained = [0]

    def drain(upto):
        for s, ref in sends[drained[0] : upto]:
            pltpu.make_async_copy(ref, ref, ssem.at[s]).wait()
        drained[0] = upto

    def gather_col_start(rnd, *cuts):
        buf = col_src[rnd]
        runs = [(pl.ds(*cut), new_recv(nz), new_send(buf.at[0 : nz - 1, 0, pl.ds(*cut)])) for cut in cuts]
        return runs, new_recv(), new_send(buf.at[:, 0])

    def gather_col_run(rnd, sems, i):
        buf = col_src[rnd]
        runs, c_recv, c_send = sems
        some, z_recv, s = runs[i]
        for d in near_first(nz):
            push(buf.at[z, core, some], buf.at[z, core, some], z_at(d)[1], s, z_recv + d)
        push(buf.at[z, core, some], buf.at[z, core, some], sibling, c_send, c_recv)

    def gather_col_pass(rnd, sems, d):
        buf = col_src[rnd]
        runs, c_recv, c_send = sems
        src = (z + nz - d) % nz
        for some, z_recv, _ in runs:
            landed(z_recv + d, buf.at[src, core, some])
        push(buf.at[src, core], buf.at[src, core], sibling, c_send, c_recv)

    def gather_col_finish(rnd, sems):
        landed(sems[1], col_src[rnd].at[:, 0])

    def gather_row_start():
        y_recv = new_recv(ny)
        s = new_send(row_src.at[0 : ny - 1, 0, low])
        for d in near_first(ny):
            push(row_src.at[y, x, low], row_src.at[y, x, low], y_at(d)[1], s, y_recv + d)
        x_recv = new_recv()
        s = new_send(row_src.at[0, 0 : nx - 1])
        for d in near_first(nx):
            push(row_src.at[y, x], row_src.at[y, x], x_at(d)[1], s, x_recv)
        return y_recv, x_recv, new_recv(), new_send(row_src.at[0 : ny - 1, 0 : nx - 1, low])

    def gather_row_high(sems):
        landed(sems[1], row_src.at[0, 0 : nx - 1])
        r = new_recv()
        s = new_send(row_src.at[0 : ny - 1, :, high])
        for d in near_first(ny):
            push(row_src.at[y, :, high], row_src.at[y, :, high], y_at(d)[1], s, r)
        return r

    def gather_row_pass(sems, d):
        y_recv, _, r, s = sems
        src = (y + ny - d) % ny
        landed(y_recv + d, row_src.at[src, x, low])
        for e in far_first(nx):
            push(row_src.at[src, x, low], row_src.at[src, x, low], x_at(e)[1], s, r)

    def gather_row_finish(sems, high_recv):
        landed(sems[2], row_src.at[0 : ny - 1, 0 : nx - 1, low])
        landed(high_recv, row_src.at[0 : ny - 1, :, high])

    unroll = 32

    def spread_forward(rnd):
        src = col_src[rnd]

        def some(turn, acc):
            for i in range(unroll):
                k = turn * unroll + i
                c = meta[1, k]
                d = jnp.dot(tiles[meta[0, k]], src[c // 2, c % 2], preferred_element_type=F32)
                acc = acc * meta[2, k].astype(F32) + d
                part[k] = acc.astype(BF)
            return acc

        lax.fori_loop(0, slots // unroll, some, jnp.zeros((height, height), F32))

        def place(b, _):
            send_f[rnd, b // nx, b % nx] = part[meta[3, b]]
            return 0

        lax.fori_loop(0, nx * ny, place, 0, unroll=8)

    def spread_backward():
        def some(turn, acc):
            for i in range(unroll):
                k = turn * unroll + i
                r = meta[5, k]
                d = jnp.dot(row_src[r // nx, r % nx], tiles[meta[4, k]], preferred_element_type=F32)
                acc = acc * meta[6, k].astype(F32) + d
                part[k] = acc.astype(BF)
            return acc

        lax.fori_loop(0, slots // unroll, some, jnp.zeros((height, height), F32))

        def place(b, _):
            send_b[b // 2, b % 2] = part[meta[7, b]]
            return 0

        lax.fori_loop(0, nz * 2, place, 0, unroll=8)

    y_turns = far_first(ny) + [0]

    def reduce_rows_start(rnd):
        buf = send_f.at[rnd]
        b_recv, b_send = new_recv(), new_send(ry_b.at[rnd, 0 : ny - 1])
        sems = []
        for j, (first, count) in enumerate(pieces[rnd]):
            a_recv, a_send = new_recv(ny), new_send(rx_a.at[rnd, :, 0 : nx - 1, pl.ds(first, count)])
            for i, dy in enumerate(y_turns):
                for dx in far_first(nx):
                    px, peer = x_at(dx)
                    push(
                        buf.at[(y + dy) % ny, px, pl.ds(rest + first, count)],
                        rx_a.at[rnd, dy, x, pl.ds(first, count)], peer, a_send, a_recv + dy,
                    )
                if i < ny - 1 and j == 0:
                    py, peer = y_at(dy)
                    push(buf.at[py, :, high], ry_b.at[rnd, y], peer, b_send, b_recv)
            sems.append((a_recv, new_recv(), new_send(ry_a.at[rnd, 0 : ny - 1, pl.ds(first, count)])))
        return sems, b_recv

    def reduce_rows_pass(rnd, sems, dy, j=0):
        a_recv, ya_recv, ya_send = sems[0][j]
        first, count = pieces[rnd][j]
        some = pl.ds(first, count)
        landed(a_recv + dy, rx_a.at[rnd, dy, 0 : nx - 1, some])
        total = send_f[rnd, (y + dy) % ny, x, pl.ds(rest + first, count)].astype(F32)
        for dx in near_first(nx):
            total += rx_a[rnd, dy, (x + dx) % nx, some].astype(F32)
        if dy == 0:
            mid_a[rnd, 0, some] = total
        else:
            mid = ry_a.at[rnd, ny + dy, some]
            mid[...] = total.astype(BF)
            push(mid, ry_a.at[rnd, y, some], y_at(dy)[1], ya_send, ya_recv)

    def reduce_rows_high(rnd, sems):
        landed(sems[1], ry_b.at[rnd, 0 : ny - 1])
        r, s = new_recv(), new_send(rx_b.at[rnd, 0 : nx - 1])
        for dx in far_first(nx) + [0]:
            px = (x + dx) % nx
            total = send_f[rnd, y, px, 0:rest].astype(F32)
            for dy in near_first(ny):
                total += ry_b[rnd, (y + dy) % ny, px].astype(F32)
            if dx == 0:
                mid_b[rnd, 0] = total
            else:
                mid = rx_b.at[rnd, nx + dx]
                mid[...] = total.astype(BF)
                push(mid, rx_b.at[rnd, x], x_at(dx)[1], s, r)
        return r

    def reduce_rows_finish_high(rnd, high_recv):
        landed(high_recv, rx_b.at[rnd, 0 : nx - 1])
        total = mid_b[rnd, 0]
        for dx in near_first(nx):
            total += rx_b[rnd, (x + dx) % nx].astype(F32)
        return total

    def reduce_rows_finish_low(rnd, sems, j=0):
        first, count = pieces[rnd][j]
        some = pl.ds(first, count)
        landed(sems[0][j][1], ry_a.at[rnd, 0 : ny - 1, some])
        total = mid_a[rnd, 0, some]
        for dy in near_first(ny):
            total += ry_a[rnd, (y + dy) % ny, some].astype(F32)
        return total

    def reduce_cols_start():
        r = new_recv()
        push(send_b.at[:, 1 - core], r_core, sibling, new_send(r_core), r)
        return r

    def reduce_cols_second(recv):
        landed(recv, r_core)
        r, s = new_recv(), new_send(r_z.at[0 : nz - 1])
        for d in near_first(nz):
            pz, peer = z_at(d)
            mid_z[pz] = (send_b[pz, core].astype(F32) + r_core[pz].astype(F32)).astype(BF)
            push(mid_z.at[pz], r_z.at[z], peer, s, r)
        return r

    def reduce_cols_finish(recv):
        total = send_b[z, core].astype(F32) + r_core[z].astype(F32)
        landed(recv, r_z.at[0 : nz - 1])
        for d in near_first(nz):
            total += r_z[(z + d) % nz].astype(F32)
        return total.astype(BF)

    part[slots] = jnp.zeros((height, height), BF)
    loads["cot"].wait()
    loads["own"].wait()
    row_src[y, x] = cot[...].astype(F32).T.astype(BF)
    pl.semaphore_wait(barrier, len(everyone))

    col_sems = gather_col_start(0, (0, height))
    gather_col_run(0, col_sems, 0)
    row_sems = gather_row_start()
    loads["rows"].wait()
    loads["cols"].wait()
    loads["count"].wait()
    live = count[0, 0]
    meta_v[...] = jnp.zeros_like(meta_v)
    for i, line in enumerate(slot_order(rows[0], cols[0], live, nx * ny) + slot_order(cols[0], rows[0], live, nz * 2)):
        meta_v[i : i + 1, 0:slots] = line
    meta_copy = pltpu.make_async_copy(meta_v, meta, local_sem.at[8])
    meta_copy.start()
    high_recv = gather_row_high(row_sems)
    for i in range(1, max(ny, nz)):
        if i < nz:
            gather_col_pass(0, col_sems, near_first(nz)[i - 1])
        if i < ny:
            gather_row_pass(row_sems, near_first(ny)[i - 1])
    meta_copy.wait()
    loads["tiles"].wait()
    gather_col_finish(0, col_sems)
    spread_forward(0)
    sum_sems = reduce_rows_start(0)
    gather_row_finish(row_sems, high_recv)
    spread_backward()
    core_recv = reduce_cols_start()
    for dy in y_turns[0:2]:
        reduce_rows_pass(0, sum_sems, dy)
    z_recv = reduce_cols_second(core_recv)
    for dy in y_turns[2:]:
        reduce_rows_pass(0, sum_sems, dy)
    for dy in y_turns[:2]:
        reduce_rows_pass(0, sum_sems, dy, 1)
    high_recv = reduce_rows_high(0, sum_sems)
    for dy in y_turns[2:7]:
        reduce_rows_pass(0, sum_sems, dy, 1)
    loads["w_in"].wait()
    loads["w_hid"].wait()

    col_sems = gather_col_start(1, (0, early), (early, height - early))

    def activate(mixed):
        sums = split_dot(mixed, w_in[...])
        return sums, (sums / (1.0 + jnp.exp(-sums))).astype(BF)

    mixed_high = reduce_rows_finish_high(0, high_recv)
    mixed_early = jnp.concatenate([mixed_high, reduce_rows_finish_low(0, sum_sems, 0)], axis=0)
    sum_early, hidden_early = activate(mixed_early)
    col_src_1[z, core, 0:early] = hidden_early
    gather_col_run(1, col_sems, 0)
    for dy in y_turns[7:]:
        reduce_rows_pass(0, sum_sems, dy, 1)
    mixed_late = reduce_rows_finish_low(0, sum_sems, 1)
    sum_late, hidden_late = activate(mixed_late)
    col_src_1[z, core, early:height] = hidden_late
    gather_col_run(1, col_sems, 1)
    mixed = jnp.concatenate([mixed_early, mixed_late], axis=0)
    sum_first = jnp.concatenate([sum_early, sum_late], axis=0)

    mixed_t = mixed.T.astype(BF)
    sum_t = sum_first.T
    gate_t = 1.0 / (1.0 + jnp.exp(-sum_t))
    hidden_t = (sum_t * gate_t).astype(BF)
    slope_t = gate_t * (1.0 + sum_t * (1.0 - gate_t))
    grad_t = reduce_cols_finish(z_recv)
    grad_sum_t = (jnp.dot(w_hid[...], grad_t, preferred_element_type=F32) * slope_t).astype(BF)
    term[0:height] = lax.dot_general(mixed_t, grad_sum_t, CONTRACT_LAST, preferred_element_type=F32).astype(BF)
    term[height : 2 * height] = lax.dot_general(
        hidden_t, grad_t, CONTRACT_LAST, preferred_element_type=F32
    ).astype(BF)
    band = 2 * height // nx

    def rows_of(i):
        return pl.ds(pl.multiple_of(i * band, band), band)

    r_x, s_x = new_recv(), new_send(ar_x.at[0 : nx - 1])
    for d in far_first(nx):
        push(term.at[rows_of(x_at(d)[0])], ar_x.at[x], x_at(d)[1], s_x, r_x)
    for d in near_first(nz)[0:3]:
        gather_col_pass(1, col_sems, d)
    landed(r_x, ar_x.at[0 : nx - 1])
    total = term[rows_of(x)].astype(F32)
    for d in near_first(nx):
        total += ar_x[(x + d) % nx].astype(F32)
    ar_y[y] = total.astype(BF)
    r_y, s_y = new_recv(), new_send(ar_y.at[0 : ny - 1])
    for d in far_first(ny):
        push(ar_y.at[y], ar_y.at[y], y_at(d)[1], s_y, r_y)
    for d in near_first(nz)[3:]:
        gather_col_pass(1, col_sems, d)
    gather_col_finish(1, col_sems)
    spread_forward(1)
    before = len(sends)
    sum_sems = reduce_rows_start(1)
    landed(r_y, ar_y.at[0 : ny - 1])
    total = ar_y[0].astype(F32)
    for i in range(1, ny):
        total += ar_y[i].astype(F32)
    ar_core[core] = total.astype(BF)
    r_core_sum = new_recv()
    push(ar_core.at[core], ar_core.at[core], sibling, new_send(ar_core.at[0]), r_core_sum)
    for dy in y_turns[0:1]:
        reduce_rows_pass(1, sum_sems, dy)
    landed(r_core_sum, ar_core.at[0])
    ar_z[z] = (ar_core[0].astype(F32) + ar_core[1].astype(F32)).astype(BF)
    r_last, s_last = new_recv(), new_send(ar_z.at[0 : nz - 1])
    for d in far_first(nz):
        push(ar_z.at[z], ar_z.at[z], z_at(d)[1], s_last, r_last)
    for dy in y_turns[1:-2]:
        reduce_rows_pass(1, sum_sems, dy)
    high_recv = reduce_rows_high(1, sum_sems)
    for dy in y_turns[-2:]:
        reduce_rows_pass(1, sum_sems, dy)
    landed(r_last, ar_z.at[0 : nz - 1])
    total = ar_z[0].astype(F32)
    for i in range(1, nz):
        total += ar_z[i].astype(F32)
    ar_out[rows_of(x)] = total.astype(BF)
    r_out, s_out = new_recv(), new_send(ar_out.at[0 : 2 * height - band])
    for d in far_first(nx):
        push(ar_out.at[rows_of(x)], ar_out.at[rows_of(x)], x_at(d)[1], s_out, r_out)
    drain(before)
    mixed = jnp.concatenate([reduce_rows_finish_high(1, high_recv), reduce_rows_finish_low(1, sum_sems)], axis=0)
    logits[...] = split_dot(mixed, w_hid[...])
    landed(r_out, ar_out.at[0 : 2 * height - band])
    gw_in[...] = ar_out[0:height].astype(F32)
    gw_hid[...] = ar_out[height : 2 * height].astype(F32)

    drain(len(sends))


def write_out(a, b, c, a_out, b_out, c_out, sem):
    copies = [pltpu.make_async_copy(s, d, sem.at[i]) for i, (s, d) in enumerate([(a, a_out), (b, b_out), (c, c_out)])]
    for copy in copies:
        copy.start()
    for copy in copies:
        copy.wait()


def body(nx, features, weight_in, weight_hidden, tile_rows, tile_cols, tile_values, tile_counts, cotangent):
    nz = lax.axis_size("row") // 2
    ny = lax.axis_size(("col", "rep")) // nx
    slots, height = tile_values.shape[2], tile_values.shape[3]
    rest = height - CUT
    band = 2 * height // nx
    block = (height, height)
    vmem = pl.BlockSpec(memory_space=pltpu.VMEM)
    hbm = pl.BlockSpec(memory_space=pltpu.HBM)
    results = [jax.ShapeDtypeStruct(block, F32)] * 3
    outs = pl.pallas_call(
        functools.partial(kernel, nx, ny, nz, slots),
        out_shape=results,
        in_specs=[hbm] * 8,
        out_specs=[vmem] * 3,
        scratch_shapes=[
            pltpu.VMEM(block, BF),
            pltpu.VMEM(block, BF),
            pltpu.VMEM((1, 1, slots), I32),
            pltpu.VMEM((1, 1, slots), I32),
            pltpu.VMEM((slots,) + block, BF),
            pltpu.SMEM((1, 1), I32),
            pltpu.VMEM(block, BF),
            pltpu.VMEM((8, 128), I32),
            pltpu.SMEM((8, 128), I32),
            pltpu.VMEM((nz, 2) + block, BF),
            pltpu.VMEM((nz, 2) + block, BF),
            pltpu.VMEM((ny, nx) + block, BF),
            pltpu.VMEM((slots + 1,) + block, BF),
            pltpu.VMEM((2, ny, nx) + block, BF),
            pltpu.VMEM((2, ny, nx, CUT, height), BF),
            pltpu.VMEM((2, 2 * nx, rest, height), BF),
            pltpu.VMEM((2, 1, CUT, height), F32),
            pltpu.VMEM((2, 1, rest, height), F32),
            pltpu.VMEM((2, 2 * ny, CUT, height), BF),
            pltpu.VMEM((2, ny, nx, rest, height), BF),
            pltpu.VMEM((nz, 2) + block, BF),
            pltpu.VMEM((nz,) + block, BF),
            pltpu.VMEM((nz,) + block, BF),
            pltpu.VMEM((nz,) + block, BF),
            pltpu.VMEM((2 * height, height), BF),
            pltpu.VMEM((nx, band, height), BF),
            pltpu.VMEM((ny, band, height), BF),
            pltpu.VMEM((2, band, height), BF),
            pltpu.VMEM((nz, band, height), BF),
            pltpu.VMEM((2 * height, height), BF),
            pltpu.SemaphoreType.DMA((9,)),
            pltpu.SemaphoreType.DMA((48,)),
            pltpu.SemaphoreType.DMA((88,)),
        ],
        compiler_params=pltpu.CompilerParams(
            collective_id=0, has_side_effects=True, vmem_limit_bytes=56 * 1024 * 1024
        ),
    )(
        features, weight_in, weight_hidden, tile_rows, tile_cols,
        tile_values.reshape((slots,) + block), tile_counts, cotangent,
    )
    return pl.pallas_call(
        write_out,
        out_shape=results,
        in_specs=[vmem] * 3,
        out_specs=[hbm] * 3,
        scratch_shapes=[pltpu.SemaphoreType.DMA((3,))],
    )(*outs)


def solution(mesh, nx=4):
    return jax.shard_map(
        functools.partial(body, nx),
        mesh=mesh,
        in_specs=(
            P(("row", "col", "rep"), None),
            P(),
            P(),
            P("row", ("col", "rep"), None),
            P("row", ("col", "rep"), None),
            P("row", ("col", "rep"), None, None, None),
            P("row", ("col", "rep")),
            P(("row", "col", "rep"), None),
        ),
        out_specs=(P(("row", "col", "rep"), None), P(), P()),
        check_vma=False,
    )
```
